32 devices in a mesh: section: 2 (over x), dp: 4 (over y, core), tensor: 4 (over z).
Axes of the slice: x: 2, y: 2, z: 4, core: 2. Of those that a mesh axis runs over, the one named last changes fastest.
Arguments:
- tokens_in: bfloat16 [2, 7168, 1024], P(None, 'tensor', 'dp'), may hold values from -47 to 47
- section_proj: bfloat16 [2, 7168, 7168], P('section', 'tensor'), may hold values from -0.0625 to 0.0625
- section_gain: bfloat16 [2, 7168], P('section', 'tensor'), may hold values from 0.099609375 to 1.8984375
- final_gain: bfloat16 [7168], P('tensor'), may hold values from 0.099609375 to 1.8984375
- score_weight: bfloat16 [7168], P('tensor'), may hold values from -0.0625 to 0.0625
- labels: int32 [2, 1024], P(None, 'dp'), may hold values from 0 to 2
- loss_mask: int32 [2, 1024], P(None, 'dp'), may hold values 0 or 1
- segment_ids: int32 [2, 1024], P(None, 'dp'), may hold values from 0 to 15, never falling along the last dimension, each value on 1 to 512 neighbouring positions
Outputs:
- section_out: bfloat16 [2, 2, 7168, 1024], P('section', None, 'tensor', 'dp')
- segment_loss: float32 [2, 16], replicated
The draws below stay inside these ranges and needn't reach their ends.
Inputs may be any that keep to these rules, and one draw needn't show every extreme that they name: `segment_ids`: within a micro-batch segment numbers never fall along the tokens; each segment has 1 to 512 tokens.
All inputs are finite; a program needn't handle non-finite values. No bound on the sum of `loss_mask` on one device may be relied on, other than what follows from the above.
Results may differ from the reference program's by a relative error of at most 0.0045.
Values may be sent and summed in bfloat16 or wider, within the bound.
A program may use at most 64 MiB of HBM per device.

```python
import math
import jax
import jax.numpy as jnp
import numpy as np
from jax import lax

D = 7168
TOK_DEV = 256
MB = 2
SEGS = 16
LEVELS = 3
TOKENS = 1024
N_SECTION = 2


def draw_tokens_in(key, part):
    key_base, key_rows, key_cols = jax.random.split(key, 3)
    shape = (MB, D, TOKENS)
    base = jnp.clip(jax.random.normal(key_base, shape, jnp.float32), -5.0, 5.0)
    token_scale = jnp.exp(jax.random.uniform(key_rows, (MB, 1, TOKENS), jnp.float32, math.log(0.3), math.log(3.0)))
    feature_scale = jnp.exp(jax.random.uniform(key_cols, (1, D, 1), jnp.float32, math.log(0.3), math.log(3.0)))
    return (base * token_scale * feature_scale).astype(jnp.bfloat16)


def set_ends(entries, key, smallest, largest):
    index_at = [jax.random.randint(jax.random.fold_in(key, axis), (), 0, length) for axis, length in enumerate(entries.shape)]
    longest = entries.shape.index(max(entries.shape))
    next_to = index_at[:longest] + [(index_at[longest] + 1) % entries.shape[longest]] + index_at[longest + 1:]
    return entries.at[tuple(index_at)].set(smallest).at[tuple(next_to)].set(largest)


def shard_levels(rng, dims, cuts, low, top_value):
    loudness = 1.0
    for axis_at, parts in cuts:
        heights = jax.random.uniform(jax.random.fold_in(jax.random.fold_in(rng, 6), axis_at), (parts,), jnp.float32, low / len(cuts), top_value / len(cuts))
        loudness = loudness * jnp.repeat(jnp.exp(heights), dims[axis_at] // parts).reshape((-1,) + (1,) * (len(dims) - 1 - axis_at))
    return loudness


def split_up(amount, total, limit, skew):
    weights = [(1 << 20) // math.isqrt(standing ** skew) + 1 for standing in range(2, amount + 1)]
    surplus, counts = total - limit - (amount - 1), [1] * (amount - 1)
    while surplus > 0:
        candidates = [i for i in range(amount - 1) if counts[i] < limit]
        whole, budget = sum([weights[i] for i in candidates]), surplus
        for i in candidates:
            more = min(limit - counts[i], max(1, budget * weights[i] // whole), surplus)
            counts[i] = counts[i] + more
            surplus = surplus - more
    return np.array([limit] + counts)


def ragged_sizes(rng, count, total, most, slope):
    if count == 2:
        one = jax.random.randint(rng, (), max(1, total - most), min(most, total - 1) + 1)
        return jnp.stack([one, total - one])
    tallies = jnp.asarray(split_up(count, total, most, slope), jnp.int32)
    couples = (count - 1) // 2
    source_of, sink = tallies[1:1 + 2 * couples:2], tallies[2:2 + 2 * couples:2]
    margin = jnp.minimum(source_of - 1, most - sink)
    moved = jax.random.randint(jax.random.fold_in(rng, 1), (couples,), 0, 1 << 20) % (margin + 1)
    tallies = tallies.at[1:1 + 2 * couples:2].set(source_of - moved).at[2:2 + 2 * couples:2].set(sink + moved)
    return tallies[jax.random.permutation(jax.random.fold_in(rng, 2), count)]


def gaussian(key, extent, width, bound, pieces=(), kind=jnp.bfloat16):
    entries = width * jax.random.normal(key, extent, jnp.float32)
    if pieces:
        entries = entries * shard_levels(key, extent, pieces, -0.22, 0.18)
    return jnp.clip(entries, -bound, bound).astype(kind)


def setup_inputs(seed: int = 0) -> dict:
    splits = jax.random.split(jax.random.key(seed), 9)
    tokens_in = draw_tokens_in(jax.random.fold_in(splits[8], 71), 0)
    section_proj = gaussian(splits[1], (N_SECTION, D, D), D ** -0.5, 0.0625, ((0, 2), (1, 4)))
    section_gain = jnp.clip(1.0 + 0.18 * jax.random.normal(splits[2], (N_SECTION, D), jnp.float32), 0.099609375, 1.8984375).astype(jnp.bfloat16)
    final_gain = jnp.clip(1.0 + 0.18 * jax.random.normal(splits[3], (D,), jnp.float32), 0.099609375, 1.8984375).astype(jnp.bfloat16)
    score_weight = gaussian(splits[4], (D,), D ** -0.5, 0.0625, ((0, 4),))
    labels = set_ends(jax.random.randint(splits[5], (MB, TOKENS), 0, LEVELS), jax.random.fold_in(splits[5], 1), 0, LEVELS - 1).astype(jnp.int32)
    loss_mask = set_ends((jax.random.randint(splits[6], (MB, TOKENS), 0, 2) < 1).astype(jnp.int32), jax.random.fold_in(splits[6], 1), 0, 1)
    segment_ids = jax.vmap(lambda own: jnp.searchsorted(jnp.cumsum(ragged_sizes(own, SEGS, TOKENS, 2 * TOK_DEV, 2)), jnp.arange(TOKENS), side="right"))(jax.random.split(splits[7], MB)).reshape((MB, TOKENS)).astype(jnp.int32)
    return dict(tokens_in=tokens_in, section_proj=section_proj, section_gain=section_gain, final_gain=final_gain, score_weight=score_weight, labels=labels, loss_mask=loss_mask, segment_ids=segment_ids)


epsilon = 1e-05

def apply_block(rows_in, weight, gain):
    as_float = rows_in.astype(jnp.float32)
    inv_root = lax.rsqrt(lax.optimization_barrier(jnp.mean(as_float * as_float, axis=-1, keepdims=True)) + epsilon)
    normed = (as_float * inv_root * gain.astype(jnp.float32)).astype(jnp.bfloat16)
    mixed = jnp.dot(normed, weight.T, preferred_element_type=jnp.float32)
    return (as_float + jax.nn.silu(mixed)).astype(jnp.bfloat16)

def reference(tokens_in, section_proj, section_gain, final_gain, score_weight, labels, loss_mask, segment_ids):
    first_rows = []
    second_rows = []
    loss_rows = []
    segment_range = jnp.arange(SEGS, dtype=jnp.int32)
    head_vector = final_gain.astype(jnp.float32) * score_weight.astype(jnp.float32)
    for micro in range(MB):
        after_first = apply_block(tokens_in[micro].T, section_proj[0], section_gain[0])
        after_second = apply_block(after_first, section_proj[1], section_gain[1])
        first_rows.append(after_first.T)
        second_rows.append(after_second.T)
        as_float = after_second.astype(jnp.float32)
        inv_root = lax.rsqrt(lax.optimization_barrier(jnp.mean(as_float * as_float, axis=-1)) + epsilon)
        scores = lax.optimization_barrier(jnp.sum(as_float * head_vector[None, :], axis=-1)) * inv_root
        target = labels[micro].astype(jnp.float32) - 1.0
        weight_mask = loss_mask[micro].astype(jnp.float32)
        offset_err = scores - target
        squared = weight_mask * offset_err * offset_err
        member = (segment_ids[micro][:, None] == segment_range[None, :]).astype(jnp.float32)
        loss_sums = jnp.dot(squared, member, precision=lax.Precision.HIGHEST)
        counted = jnp.dot(weight_mask, member, precision=lax.Precision.HIGHEST)
        loss_rows.append(loss_sums / jnp.maximum(counted, 1.0))
    section_out = jnp.stack([jnp.stack(first_rows), jnp.stack(second_rows)])
    return (section_out, jnp.stack(loss_rows))
```

```python
import functools

import jax
import jax.numpy as jnp
from jax import lax
from jax.experimental import pallas as pl
from jax.experimental.pallas import tpu as pltpu
from jax.sharding import PartitionSpec as P

SEGS = 16
LANES = 128
epsilon = 1e-05
MESH = pl.DeviceIdType.MESH


def each(low, high, step):
    if high - low <= 8:
        for i in range(low, high):
            step(i)
    else:
        lax.fori_loop(low, high, lambda i, _: (step(i), 0)[1], 0)


def row_tile(rows):
    return next(t for t in range(256, 0, -16) if rows % t == 0)


def kernel(
    tensor_n,
    dp_n,
    micros,
    width,
    rows,
    tok_ref,
    w_ref,
    cols_ref,
    labels_ref,
    mask_ref,
    seg_ref,
    out_ref,
    loss_ref,
    w,
    x,
    g,
    sq,
    o,
    parts,
    lc,
    w_sem,
    tok_sem,
    out_sem,
    g_send,
    g_recv,
    q_send,
    q_recv,
    x_send,
    x_recv,
    p_send,
    p_recv,
    l_send,
    l_recv,
):
    chunks = x.shape[0]
    per_micro = chunks // micros
    tile = row_tile(rows)
    tiles = rows // tile
    sec = lax.axis_index("section")
    dp = lax.axis_index("dp")
    me = lax.axis_index("tensor")
    group = 2 * dp_n
    place = sec * dp_n + dp

    def around(d):
        return lax.rem(me + d, tensor_n)

    def cousin(k):
        there = lax.rem(place + k, group)
        return {"section": there // dp_n, "dp": lax.rem(there, dp_n)}

    barrier = pltpu.get_barrier_semaphore()
    each(
        1,
        tensor_n,
        lambda d: pl.semaphore_signal(
            barrier, inc=1, device_id={"tensor": around(d)}, device_id_type=MESH
        ),
    )
    each(
        1,
        group,
        lambda k: pl.semaphore_signal(
            barrier, inc=1, device_id=cousin(k), device_id_type=MESH
        ),
    )

    load_w = pltpu.make_async_copy(w_ref, w, w_sem)

    def load_tok(c):
        return pltpu.make_async_copy(
            tok_ref.at[c // per_micro, :, pl.ds((c % per_micro) * LANES, LANES)],
            x.at[c],
            tok_sem.at[c],
        )

    def store_out(c):
        return pltpu.make_async_copy(
            o.at[c],
            out_ref.at[c // per_micro, :, pl.ds((c % per_micro) * LANES, LANES)],
            out_sem.at[c],
        )

    def block(c, owner):
        return g.at[c, pl.ds(pl.multiple_of(owner * rows, 16), rows), :]

    def gather_copy(c, owner, peer, d):
        return pltpu.make_async_remote_copy(
            src_ref=block(c, owner),
            dst_ref=block(c, owner),
            send_sem=g_send.at[c, d],
            recv_sem=g_recv.at[c, owner],
            device_id={"tensor": peer},
            device_id_type=MESH,
        )

    def square_copy(c, owner, peer, d):
        return pltpu.make_async_remote_copy(
            src_ref=sq.at[c, owner],
            dst_ref=sq.at[c, owner],
            send_sem=q_send.at[c, d],
            recv_sem=q_recv.at[c, owner],
            device_id={"tensor": peer},
            device_id_type=MESH,
        )

    def part_copy(c, owner, peer, d):
        return pltpu.make_async_remote_copy(
            src_ref=parts.at[c, owner],
            dst_ref=parts.at[c, owner],
            send_sem=p_send.at[c, d],
            recv_sem=p_recv.at[c, owner],
            device_id={"tensor": peer},
            device_id_type=MESH,
        )

    def handoff(c):
        return pltpu.make_async_remote_copy(
            src_ref=o.at[c],
            dst_ref=x.at[c],
            send_sem=x_send.at[c],
            recv_sem=x_recv.at[c],
            device_id={"section": 1 - sec},
            device_id_type=MESH,
        )

    def loss_copy(owner, k):
        return pltpu.make_async_remote_copy(
            src_ref=lc.at[owner],
            dst_ref=lc.at[owner],
            send_sem=l_send.at[k],
            recv_sem=l_recv.at[owner],
            device_id=cousin(k),
            device_id_type=MESH,
        )

    @pl.when(sec == 0)
    def _():
        for c in range(chunks):
            load_tok(c).start()

    load_w.start()
    pl.semaphore_wait(barrier, tensor_n - 1 + group - 1)

    def ready(c):
        @pl.when(sec == 0)
        def _():
            load_tok(c).wait()

        @pl.when(sec == 1)
        def _():
            handoff(c).wait_recv()

    def folded(v):
        return jnp.sum(v.reshape(v.shape[0] // 8, 8, LANES), axis=0)

    def prepare(c):
        def step(i, total):
            at = pl.multiple_of(i * tile, 16)
            v = x[c, pl.ds(at, tile), :].astype(jnp.float32)
            gain = cols_ref[pl.ds(at, tile), 0:1]
            g[c, pl.ds(pl.multiple_of(me * rows + at, 16), tile), :] = (v * gain).astype(
                jnp.bfloat16
            )
            return total + folded(v * v)

        sq[c, me] = lax.fori_loop(0, tiles, step, jnp.zeros((8, LANES), jnp.float32))

    def send(c):
        def one(d):
            square_copy(c, me, around(d), d).start()
            gather_copy(c, me, around(d), d).start()

        each(1, tensor_n, one)

    def sent(c):
        def one(d):
            square_copy(c, me, around(d), d).wait_send()
            gather_copy(c, me, around(d), d).wait_send()

        each(1, tensor_n, one)

    def arrived(c):
        def one(d):
            square_copy(c, around(d), around(d), d).wait_recv()
            gather_copy(c, around(d), around(d), d).wait_recv()

        each(1, tensor_n, one)

    def over_tensor(ref, c, low):
        total = ref[c, 0, low : low + 8, :]
        for t in range(1, tensor_n):
            total = total + ref[c, t, low : low + 8, :]
        return jnp.sum(total, axis=0, keepdims=True)

    def compute(c):
        q = lax.rsqrt(over_tensor(sq, c, 0) / width + epsilon)

        def step(i, totals):
            at = pl.multiple_of(i * tile, 16)
            mixed = q * jnp.dot(
                w[pl.ds(at, tile), :], g[c], preferred_element_type=jnp.float32
            )
            v = x[c, pl.ds(at, tile), :].astype(jnp.float32)
            result = (v + mixed / (1.0 + jnp.exp(-mixed))).astype(jnp.bfloat16)
            o[c, pl.ds(at, tile), :] = result
            f = result.astype(jnp.float32)
            head = cols_ref[pl.ds(at, tile), 1:2]
            return totals[0] + folded(f * f), totals[1] + folded(f * head)

        zero = jnp.zeros((8, LANES), jnp.float32)
        squares, dots = lax.fori_loop(0, tiles, step, (zero, zero))
        parts[c, me, 0:8, :] = squares
        parts[c, me, 8:16, :] = dots

    ready(0)
    prepare(0)
    send(0)
    for c in range(chunks):
        if c + 1 < chunks:
            ready(c + 1)
            prepare(c + 1)
        sent(c)
        if c + 1 < chunks:
            send(c + 1)
        arrived(c)
        if c == 0:
            load_w.wait()
        compute(c)
        store_out(c).start()

        @pl.when(sec == 0)
        def _():
            handoff(c).start()

        @pl.when(sec == 1)
        def _():
            each(1, tensor_n, lambda d: part_copy(c, me, around(d), d).start())

    @pl.when(sec == 1)
    def _():
        segment = lax.broadcasted_iota(jnp.int32, (SEGS, LANES), 0)
        for m in range(micros):
            losses = jnp.zeros((SEGS, LANES), jnp.float32)
            counts = jnp.zeros((SEGS, LANES), jnp.float32)
            for h in range(per_micro):
                c = m * per_micro + h
                each(
                    1,
                    tensor_n,
                    lambda d: part_copy(c, around(d), around(d), d).wait_recv(),
                )
                cut = slice(h * LANES, (h + 1) * LANES)
                inv_root = lax.rsqrt(over_tensor(parts, c, 0) / width + epsilon)
                scores = over_tensor(parts, c, 8) * inv_root
                weight = mask_ref[m : m + 1, cut].astype(jnp.float32)
                off = scores - (labels_ref[m : m + 1, cut].astype(jnp.float32) - 1.0)
                member = seg_ref[m : m + 1, cut] == segment
                losses += jnp.where(member, weight * off * off, 0.0)
                counts += jnp.where(member, weight, 0.0)
            lc[dp, m * SEGS : (m + 1) * SEGS, :] = losses
            lc[dp, (micros + m) * SEGS : (micros + m + 1) * SEGS, :] = counts
        each(1, group, lambda k: loss_copy(dp, k).start())
        each(1, dp_n, lambda k: loss_copy(lax.rem(dp + k, dp_n), k).wait_recv())

    @pl.when(sec == 0)
    def _():
        each(0, dp_n, lambda k: loss_copy(lax.rem(dp + k, dp_n), 1 + k).wait_recv())

    total = lc[0]
    for k in range(1, dp_n):
        total = total + lc[k]
    total = jnp.sum(total, axis=1, keepdims=True)
    half = micros * SEGS
    loss = total[:half] / jnp.maximum(total[half:], 1.0)
    loss_ref[...] = jnp.broadcast_to(loss, loss_ref.shape)

    for c in range(chunks):
        store_out(c).wait()

    @pl.when(sec == 0)
    def _():
        for c in range(chunks):
            handoff(c).wait_send()

    @pl.when(sec == 1)
    def _():
        for c in range(chunks):
            each(1, tensor_n, lambda d: part_copy(c, me, around(d), d).wait_send())
        each(1, group, lambda k: loss_copy(dp, k).wait_send())


def body(
    tensor_n,
    dp_n,
    tokens_in,
    section_proj,
    section_gain,
    final_gain,
    score_weight,
    labels,
    loss_mask,
    segment_ids,
):
    micros, rows, tokens = tokens_in.shape
    width = section_proj.shape[2]
    chunks = micros * (tokens // LANES)
    cols = jnp.stack(
        [
            section_gain[0].astype(jnp.float32),
            final_gain.astype(jnp.float32) * score_weight.astype(jnp.float32),
        ],
        axis=1,
    )
    dma = pltpu.SemaphoreType.DMA
    vmem = pl.BlockSpec(memory_space=pltpu.VMEM)
    hbm = pl.BlockSpec(memory_space=pl.ANY)
    out, loss = pl.pallas_call(
        functools.partial(kernel, tensor_n, dp_n, micros, width, rows),
        out_shape=(
            jax.ShapeDtypeStruct((micros, rows, tokens), jnp.bfloat16),
            jax.ShapeDtypeStruct((micros * SEGS, LANES), jnp.float32),
        ),
        in_specs=[hbm, hbm, vmem, vmem, vmem, vmem],
        out_specs=(hbm, vmem),
        scratch_shapes=[
            pltpu.VMEM((rows, width), jnp.bfloat16),
            pltpu.VMEM((chunks, rows, LANES), jnp.bfloat16),
            pltpu.VMEM((chunks, width, LANES), jnp.bfloat16),
            pltpu.VMEM((chunks, tensor_n, 8, LANES), jnp.float32),
            pltpu.VMEM((chunks, rows, LANES), jnp.bfloat16),
            pltpu.VMEM((chunks, tensor_n, 16, LANES), jnp.float32),
            pltpu.VMEM((dp_n, 2 * micros * SEGS, LANES), jnp.float32),
            dma,
            dma((chunks,)),
            dma((chunks,)),
            dma((chunks, tensor_n)),
            dma((chunks, tensor_n)),
            dma((chunks, tensor_n)),
            dma((chunks, tensor_n)),
            dma((chunks,)),
            dma((chunks,)),
            dma((chunks, tensor_n)),
            dma((chunks, tensor_n)),
            dma((2 * dp_n,)),
            dma((dp_n,)),
        ],
        compiler_params=pltpu.CompilerParams(
            collective_id=0, has_side_effects=True, vmem_limit_bytes=56 * 2**20
        ),
        cost_estimate=pl.CostEstimate(
            flops=2 * rows * width * micros * tokens,
            bytes_accessed=2 * rows * width,
            transcendentals=0,
        ),
        name="relay",
    )(tokens_in, section_proj[0], cols, labels, loss_mask, segment_ids)
    return out[None], loss[:, 0].reshape(micros, SEGS)


def solution(mesh):
    in_specs = (
        P(None, "tensor", "dp"),
        P("section", "tensor", None),
        P("section", "tensor"),
        P("tensor"),
        P("tensor"),
        P(None, "dp"),
        P(None, "dp"),
        P(None, "dp"),
    )
    out_specs = (P("section", None, "tensor", "dp"), P())
    return jax.shard_map(
        functools.partial(body, mesh.shape["tensor"], mesh.shape["dp"]),
        mesh=mesh,
        in_specs=in_specs,
        out_specs=out_specs,
        check_vma=False,
    )
```

```python
import functools

import jax
import jax.numpy as jnp
from jax import lax
from jax.experimental import pallas as pl
from jax.experimental.pallas import tpu as pltpu
from jax.sharding import PartitionSpec as P

SEGS = 16
LANES = 128
epsilon = 1e-05
MESH = pl.DeviceIdType.MESH


def each(low, high, step):
    if high - low <= 8:
        for i in range(low, high):
            step(i)
    else:
        lax.fori_loop(low, high, lambda i, _: (step(i), 0)[1], 0)


def row_tile(rows):
    return next(t for t in range(256, 0, -16) if rows % t == 0)


def kernel(
    tensor_n,
    dp_n,
    micros,
    width,
    rows,
    tok_ref,
    w_ref,
    cols_ref,
    labels_ref,
    mask_ref,
    seg_ref,
    out_ref,
    loss_ref,
    w,
    x,
    g,
    sq,
    o,
    acc,
    parts,
    lc,
    w_sem,
    tok_sem,
    out_sem,
    g_send,
    g_recv,
    q_send,
    q_recv,
    x_send,
    x_recv,
    p_send,
    p_recv,
    l_send,
    l_recv,
):
    chunks = x.shape[0]
    per_micro = chunks // micros
    tile = row_tile(rows)
    tiles = rows // tile
    band_rows = rows // 2 if rows % 32 == 0 else rows
    sec = lax.axis_index("section")
    dp = lax.axis_index("dp")
    me = lax.axis_index("tensor")
    group = 2 * dp_n
    place = sec * dp_n + dp

    def around(d):
        return lax.rem(me + d, tensor_n)

    def cousin(k):
        there = lax.rem(place + k, group)
        return {"section": there // dp_n, "dp": lax.rem(there, dp_n)}

    barrier = pltpu.get_barrier_semaphore()
    each(
        1,
        tensor_n,
        lambda d: pl.semaphore_signal(
            barrier, inc=1, device_id={"tensor": around(d)}, device_id_type=MESH
        ),
    )
    each(
        1,
        group,
        lambda k: pl.semaphore_signal(
            barrier, inc=1, device_id=cousin(k), device_id_type=MESH
        ),
    )

    load_w = pltpu.make_async_copy(w_ref, w, w_sem)

    def load_tok(c):
        return pltpu.make_async_copy(
            tok_ref.at[c // per_micro, :, pl.ds((c % per_micro) * LANES, LANES)],
            x.at[c],
            tok_sem.at[c],
        )

    def store_out(c):
        return pltpu.make_async_copy(
            o.at[c],
            out_ref.at[c // per_micro, :, pl.ds((c % per_micro) * LANES, LANES)],
            out_sem.at[c],
        )

    def block(c, owner):
        return g.at[c, pl.ds(pl.multiple_of(owner * rows, 16), rows), :]

    def gather_copy(c, owner, peer, d):
        return pltpu.make_async_remote_copy(
            src_ref=block(c, owner),
            dst_ref=block(c, owner),
            send_sem=g_send.at[c, d],
            recv_sem=g_recv.at[c, owner],
            device_id={"tensor": peer},
            device_id_type=MESH,
        )

    def square_copy(c, owner, peer, d):
        return pltpu.make_async_remote_copy(
            src_ref=sq.at[c, owner],
            dst_ref=sq.at[c, owner],
            send_sem=q_send.at[c, d],
            recv_sem=q_recv.at[c, owner],
            device_id={"tensor": peer},
            device_id_type=MESH,
        )

    def part_copy(c, owner, peer, d):
        return pltpu.make_async_remote_copy(
            src_ref=parts.at[c, owner],
            dst_ref=parts.at[c, owner],
            send_sem=p_send.at[c, d],
            recv_sem=p_recv.at[c, owner],
            device_id={"tensor": peer},
            device_id_type=MESH,
        )

    def handoff(c):
        return pltpu.make_async_remote_copy(
            src_ref=o.at[c],
            dst_ref=x.at[c],
            send_sem=x_send.at[c],
            recv_sem=x_recv.at[c],
            device_id={"section": 1 - sec},
            device_id_type=MESH,
        )

    def loss_copy(owner, k):
        return pltpu.make_async_remote_copy(
            src_ref=lc.at[owner],
            dst_ref=lc.at[owner],
            send_sem=l_send.at[k],
            recv_sem=l_recv.at[owner],
            device_id=cousin(k),
            device_id_type=MESH,
        )

    @pl.when(sec == 0)
    def _():
        for c in range(chunks):
            load_tok(c).start()

    load_w.start()
    pl.semaphore_wait(barrier, tensor_n - 1 + group - 1)

    def ready(c):
        @pl.when(sec == 0)
        def _():
            load_tok(c).wait()

        @pl.when(sec == 1)
        def _():
            handoff(c).wait_recv()

    def folded(v):
        return jnp.sum(v.reshape(v.shape[0] // 8, 8, LANES), axis=0)

    def prepare(c):
        def step(i, total):
            at = pl.multiple_of(i * tile, 16)
            v = x[c, pl.ds(at, tile), :].astype(jnp.float32)
            gain = cols_ref[pl.ds(at, tile), 0:1]
            g[c, pl.ds(pl.multiple_of(me * rows + at, 16), tile), :] = (v * gain).astype(
                jnp.bfloat16
            )
            return total + folded(v * v)

        sq[c, me] = lax.fori_loop(0, tiles, step, jnp.zeros((8, LANES), jnp.float32))

    def send(c):
        def one(d):
            square_copy(c, me, around(d), d).start()
            gather_copy(c, me, around(d), d).start()

        each(1, tensor_n, one)

    def sent(c):
        def one(d):
            square_copy(c, me, around(d), d).wait_send()
            gather_copy(c, me, around(d), d).wait_send()

        each(1, tensor_n, one)

    def arrived(c, d):
        square_copy(c, around(d), around(d), d).wait_recv()
        gather_copy(c, around(d), around(d), d).wait_recv()

    def over_tensor(ref, c, low):
        total = ref[c, 0, low : low + 8, :]
        for t in range(1, tensor_n):
            total = total + ref[c, t, low : low + 8, :]
        return jnp.sum(total, axis=0, keepdims=True)

    def multiply(c, owner, first):
        at = pl.multiple_of(owner * rows, 16)
        held = g[c, pl.ds(at, rows), :]

        def step(i, _):
            band = pl.ds(pl.multiple_of(i * band_rows, 16), band_rows)
            product = jnp.dot(
                w[band, pl.ds(pl.multiple_of(owner * rows, LANES), rows)],
                held,
                preferred_element_type=jnp.float32,
            )
            acc[band, :] = product if first else acc[band, :] + product
            return 0

        lax.fori_loop(0, rows // band_rows, step, 0)

    def multiply_all(c):
        def step(i, _):
            band = pl.ds(pl.multiple_of(i * tile, 16), tile)
            acc[band, :] = jnp.dot(
                w[band, :], g[c], preferred_element_type=jnp.float32
            )
            return 0

        lax.fori_loop(0, tiles, step, 0)

    def finish(c):
        q = lax.rsqrt(over_tensor(sq, c, 0) / width + epsilon)

        def step(i, totals):
            at = pl.multiple_of(i * tile, 16)
            mixed = q * acc[pl.ds(at, tile), :]
            v = x[c, pl.ds(at, tile), :].astype(jnp.float32)
            result = (v + mixed / (1.0 + jnp.exp(-mixed))).astype(jnp.bfloat16)
            o[c, pl.ds(at, tile), :] = result
            f = result.astype(jnp.float32)
            head = cols_ref[pl.ds(at, tile), 1:2]
            return totals[0] + folded(f * f), totals[1] + folded(f * head)

        zero = jnp.zeros((8, LANES), jnp.float32)
        squares, dots = lax.fori_loop(0, tiles, step, (zero, zero))
        parts[c, me, 0:8, :] = squares
        parts[c, me, 8:16, :] = dots

    def compute(c):
        if rows % LANES:
            each(1, tensor_n, lambda d: arrived(c, d))
            multiply_all(c)
        else:
            multiply(c, me, True)

            def one(d, _):
                arrived(c, d)
                multiply(c, around(d), False)
                return 0

            lax.fori_loop(1, tensor_n, one, 0)
        finish(c)

    ready(0)
    prepare(0)
    send(0)
    for c in range(chunks):
        if c + 1 < chunks:
            ready(c + 1)
            prepare(c + 1)
        sent(c)
        if c + 1 < chunks:
            send(c + 1)
        if c == 0:
            load_w.wait()
        compute(c)
        store_out(c).start()

        @pl.when(sec == 0)
        def _():
            handoff(c).start()

        @pl.when(sec == 1)
        def _():
            each(1, tensor_n, lambda d: part_copy(c, me, around(d), d).start())

    @pl.when(sec == 1)
    def _():
        segment = lax.broadcasted_iota(jnp.int32, (SEGS, LANES), 0)
        for m in range(micros):
            losses = jnp.zeros((SEGS, LANES), jnp.float32)
            counts = jnp.zeros((SEGS, LANES), jnp.float32)
            for h in range(per_micro):
                c = m * per_micro + h
                each(
                    1,
                    tensor_n,
                    lambda d: part_copy(c, around(d), around(d), d).wait_recv(),
                )
                cut = slice(h * LANES, (h + 1) * LANES)
                inv_root = lax.rsqrt(over_tensor(parts, c, 0) / width + epsilon)
                scores = over_tensor(parts, c, 8) * inv_root
                weight = mask_ref[m : m + 1, cut].astype(jnp.float32)
                off = scores - (labels_ref[m : m + 1, cut].astype(jnp.float32) - 1.0)
                member = seg_ref[m : m + 1, cut] == segment
                losses += jnp.where(member, weight * off * off, 0.0)
                counts += jnp.where(member, weight, 0.0)
            lc[dp, m * SEGS : (m + 1) * SEGS, :] = losses
            lc[dp, (micros + m) * SEGS : (micros + m + 1) * SEGS, :] = counts
        each(1, group, lambda k: loss_copy(dp, k).start())
        each(1, dp_n, lambda k: loss_copy(lax.rem(dp + k, dp_n), k).wait_recv())

    @pl.when(sec == 0)
    def _():
        each(0, dp_n, lambda k: loss_copy(lax.rem(dp + k, dp_n), 1 + k).wait_recv())

    total = lc[0]
    for k in range(1, dp_n):
        total = total + lc[k]
    total = jnp.sum(total, axis=1, keepdims=True)
    half = micros * SEGS
    loss = total[:half] / jnp.maximum(total[half:], 1.0)
    loss_ref[...] = jnp.broadcast_to(loss, loss_ref.shape)

    for c in range(chunks):
        store_out(c).wait()

    @pl.when(sec == 0)
    def _():
        for c in range(chunks):
            handoff(c).wait_send()

    @pl.when(sec == 1)
    def _():
        for c in range(chunks):
            each(1, tensor_n, lambda d: part_copy(c, me, around(d), d).wait_send())
        each(1, group, lambda k: loss_copy(dp, k).wait_send())


def body(
    tensor_n,
    dp_n,
    tokens_in,
    section_proj,
    section_gain,
    final_gain,
    score_weight,
    labels,
    loss_mask,
    segment_ids,
):
    micros, rows, tokens = tokens_in.shape
    width = section_proj.shape[2]
    chunks = micros * (tokens // LANES)
    cols = jnp.stack(
        [
            section_gain[0].astype(jnp.float32),
            final_gain.astype(jnp.float32) * score_weight.astype(jnp.float32),
        ],
        axis=1,
    )
    dma = pltpu.SemaphoreType.DMA
    vmem = pl.BlockSpec(memory_space=pltpu.VMEM)
    hbm = pl.BlockSpec(memory_space=pl.ANY)
    out, loss = pl.pallas_call(
        functools.partial(kernel, tensor_n, dp_n, micros, width, rows),
        out_shape=(
            jax.ShapeDtypeStruct((micros, rows, tokens), jnp.bfloat16),
            jax.ShapeDtypeStruct((micros * SEGS, LANES), jnp.float32),
        ),
        in_specs=[hbm, hbm, vmem, vmem, vmem, vmem],
        out_specs=(hbm, vmem),
        scratch_shapes=[
            pltpu.VMEM((rows, width), jnp.bfloat16),
            pltpu.VMEM((chunks, rows, LANES), jnp.bfloat16),
            pltpu.VMEM((chunks, width, LANES), jnp.bfloat16),
            pltpu.VMEM((chunks, tensor_n, 8, LANES), jnp.float32),
            pltpu.VMEM((chunks, rows, LANES), jnp.bfloat16),
            pltpu.VMEM((rows, LANES), jnp.float32),
            pltpu.VMEM((chunks, tensor_n, 16, LANES), jnp.float32),
            pltpu.VMEM((dp_n, 2 * micros * SEGS, LANES), jnp.float32),
            dma,
            dma((chunks,)),
            dma((chunks,)),
            dma((chunks, tensor_n)),
            dma((chunks, tensor_n)),
            dma((chunks, tensor_n)),
            dma((chunks, tensor_n)),
            dma((chunks,)),
            dma((chunks,)),
            dma((chunks, tensor_n)),
            dma((chunks, tensor_n)),
            dma((2 * dp_n,)),
            dma((dp_n,)),
        ],
        compiler_params=pltpu.CompilerParams(
            collective_id=0, has_side_effects=True, vmem_limit_bytes=56 * 2**20
        ),
        cost_estimate=pl.CostEstimate(
            flops=2 * rows * width * micros * tokens,
            bytes_accessed=2 * rows * width,
            transcendentals=0,
        ),
        name="relay",
    )(tokens_in, section_proj[0], cols, labels, loss_mask, segment_ids)
    return out[None], loss[:, 0].reshape(micros, SEGS)


def solution(mesh):
    in_specs = (
        P(None, "tensor", "dp"),
        P("section", "tensor", None),
        P("section", "tensor"),
        P("tensor"),
        P("tensor"),
        P(None, "dp"),
        P(None, "dp"),
        P(None, "dp"),
    )
    out_specs = (P("section", None, "tensor", "dp"), P())
    return jax.shard_map(
        functools.partial(body, mesh.shape["tensor"], mesh.shape["dp"]),
        mesh=mesh,
        in_specs=in_specs,
        out_specs=out_specs,
        check_vma=False,
    )
```

```python
import functools

import jax
import jax.numpy as jnp
from jax import lax
from jax.experimental import pallas as pl
from jax.experimental.pallas import tpu as pltpu
from jax.sharding import PartitionSpec as P

SEGS = 16
LANES = 128
epsilon = 1e-05
MESH = pl.DeviceIdType.MESH


def each(low, high, step):
    if high - low <= 8:
        for i in range(low, high):
            step(i)
    else:
        lax.fori_loop(low, high, lambda i, _: (step(i), 0)[1], 0)


def each_if(low, high, step):
    lax.fori_loop(low, high, lambda i, _: (step(i), 0)[1], 0)


def row_tile(rows):
    return next(t for t in range(256, 0, -16) if rows % t == 0)


def kernel(
    tensor_n,
    dp_n,
    micros,
    width,
    rows,
    tok_ref,
    w_ref,
    cols_ref,
    labels_ref,
    mask_ref,
    seg_ref,
    out_ref,
    loss_ref,
    w,
    x,
    g,
    sq,
    o,
    acc,
    parts,
    lc,
    w_sem,
    tok_sem,
    out_sem,
    g_send,
    g_recv,
    q_send,
    q_recv,
    x_send,
    x_recv,
    p_send,
    p_recv,
    l_send,
    l_recv,
):
    chunks = x.shape[0]
    per_micro = chunks // micros
    tile = row_tile(rows)
    tiles = rows // tile
    band_rows = rows // 2 if rows % 32 == 0 else rows
    sec = lax.axis_index("section")
    dp = lax.axis_index("dp")
    me = lax.axis_index("tensor")
    group = 2 * dp_n
    place = sec * dp_n + dp

    def around(d):
        return lax.rem(me + d, tensor_n)

    def cousin(k):
        there = lax.rem(place + k, group)
        return {"section": there // dp_n, "dp": lax.rem(there, dp_n)}

    barrier = pltpu.get_barrier_semaphore()
    each(
        1,
        tensor_n,
        lambda d: pl.semaphore_signal(
            barrier, inc=1, device_id={"tensor": around(d)}, device_id_type=MESH
        ),
    )
    each(
        1,
        group,
        lambda k: pl.semaphore_signal(
            barrier, inc=1, device_id=cousin(k), device_id_type=MESH
        ),
    )

    load_w = pltpu.make_async_copy(w_ref, w, w_sem)

    def load_tok(c):
        return pltpu.make_async_copy(
            tok_ref.at[c // per_micro, :, pl.ds((c % per_micro) * LANES, LANES)],
            x.at[c],
            tok_sem.at[c],
        )

    def store_out(c):
        return pltpu.make_async_copy(
            o.at[c],
            out_ref.at[c // per_micro, :, pl.ds((c % per_micro) * LANES, LANES)],
            out_sem.at[c],
        )

    def block(c, owner):
        return g.at[c, pl.ds(pl.multiple_of(owner * rows, 16), rows), :]

    def hop(c, owner, by, slot):
        return pltpu.make_async_remote_copy(
            src_ref=block(c, owner),
            dst_ref=block(c, owner),
            send_sem=g_send.at[c, slot],
            recv_sem=g_recv.at[c, owner],
            device_id={"tensor": lax.rem(me + by + tensor_n, tensor_n)},
            device_id_type=MESH,
        )

    def square_copy(c, owner, peer, d):
        return pltpu.make_async_remote_copy(
            src_ref=sq.at[c, owner],
            dst_ref=sq.at[c, owner],
            send_sem=q_send.at[c, d],
            recv_sem=q_recv.at[c, owner],
            device_id={"tensor": peer},
            device_id_type=MESH,
        )

    def part_copy(c, owner, peer, d):
        return pltpu.make_async_remote_copy(
            src_ref=parts.at[c, owner],
            dst_ref=parts.at[c, owner],
            send_sem=p_send.at[c, d],
            recv_sem=p_recv.at[c, owner],
            device_id={"tensor": peer},
            device_id_type=MESH,
        )

    def handoff(c):
        return pltpu.make_async_remote_copy(
            src_ref=o.at[c],
            dst_ref=x.at[c],
            send_sem=x_send.at[c],
            recv_sem=x_recv.at[c],
            device_id={"section": 1 - sec},
            device_id_type=MESH,
        )

    def loss_copy(owner, k):
        return pltpu.make_async_remote_copy(
            src_ref=lc.at[owner],
            dst_ref=lc.at[owner],
            send_sem=l_send.at[k],
            recv_sem=l_recv.at[owner],
            device_id=cousin(k),
            device_id_type=MESH,
        )

    @pl.when(sec == 0)
    def _():
        for c in range(chunks):
            load_tok(c).start()

    load_w.start()
    pl.semaphore_wait(barrier, tensor_n - 1 + group - 1)

    def ready(c):
        @pl.when(sec == 0)
        def _():
            load_tok(c).wait()

        @pl.when(sec == 1)
        def _():
            handoff(c).wait_recv()

    def folded(v):
        return jnp.sum(v.reshape(v.shape[0] // 8, 8, LANES), axis=0)

    def prepare(c):
        def step(i, total):
            at = pl.multiple_of(i * tile, 16)
            v = x[c, pl.ds(at, tile), :].astype(jnp.float32)
            gain = cols_ref[pl.ds(at, tile), 0:1]
            g[c, pl.ds(pl.multiple_of(me * rows + at, 16), tile), :] = (v * gain).astype(
                jnp.bfloat16
            )
            return total + folded(v * v)

        sq[c, me] = lax.fori_loop(0, tiles, step, jnp.zeros((8, LANES), jnp.float32))

    has_right = me + 1 < tensor_n
    has_left = me > 0

    def send(c):
        each(1, tensor_n, lambda d: square_copy(c, me, around(d), d).start())

        @pl.when(has_right)
        def _():
            hop(c, me, 1, me).start()

        @pl.when(has_left)
        def _():
            hop(c, me, -1, tensor_n).start()

    def sent(c):
        each(1, tensor_n, lambda d: square_copy(c, me, around(d), d).wait_send())

        @pl.when(has_right)
        def _():
            each_if(0, me + 1, lambda s: hop(c, s, 1, s).wait_send())

        @pl.when(has_left)
        def _():
            hop(c, me, -1, tensor_n).wait_send()
            each_if(me + 1, tensor_n, lambda s: hop(c, s, -1, s).wait_send())

    def arrived(c, j):
        @pl.when(me - j >= 0)
        def _():
            owner = me - j
            hop(c, owner, 1, owner).wait_recv()

            @pl.when(has_right)
            def _():
                hop(c, owner, 1, owner).start()

        @pl.when(me + j < tensor_n)
        def _():
            owner = me + j
            hop(c, owner, -1, owner).wait_recv()

            @pl.when(has_left)
            def _():
                hop(c, owner, -1, owner).start()

    def over_tensor(ref, c, low):
        total = ref[c, 0, low : low + 8, :]
        for t in range(1, tensor_n):
            total = total + ref[c, t, low : low + 8, :]
        return jnp.sum(total, axis=0, keepdims=True)

    def multiply(c, owner, first):
        at = pl.multiple_of(owner * rows, 16)
        held = g[c, pl.ds(at, rows), :]

        def step(i, _):
            band = pl.ds(pl.multiple_of(i * band_rows, 16), band_rows)
            product = jnp.dot(
                w[band, pl.ds(pl.multiple_of(owner * rows, LANES), rows)],
                held,
                preferred_element_type=jnp.float32,
            )
            acc[band, :] = product if first else acc[band, :] + product
            return 0

        lax.fori_loop(0, rows // band_rows, step, 0)

    def both(c, j):
        @pl.when(me - j >= 0)
        def _():
            multiply(c, me - j, False)

        @pl.when(me + j < tensor_n)
        def _():
            multiply(c, me + j, False)

    def multiply_all(c):
        def step(i, _):
            band = pl.ds(pl.multiple_of(i * tile, 16), tile)
            acc[band, :] = jnp.dot(
                w[band, :], g[c], preferred_element_type=jnp.float32
            )
            return 0

        lax.fori_loop(0, tiles, step, 0)

    def finish(c):
        q = lax.rsqrt(over_tensor(sq, c, 0) / width + epsilon)

        def step(i, totals):
            at = pl.multiple_of(i * tile, 16)
            mixed = q * acc[pl.ds(at, tile), :]
            v = x[c, pl.ds(at, tile), :].astype(jnp.float32)
            result = (v + mixed / (1.0 + jnp.exp(-mixed))).astype(jnp.bfloat16)
            o[c, pl.ds(at, tile), :] = result
            f = result.astype(jnp.float32)
            head = cols_ref[pl.ds(at, tile), 1:2]
            return totals[0] + folded(f * f), totals[1] + folded(f * head)

        zero = jnp.zeros((8, LANES), jnp.float32)
        squares, dots = lax.fori_loop(0, tiles, step, (zero, zero))
        parts[c, me, 0:8, :] = squares
        parts[c, me, 8:16, :] = dots

    def compute(c):
        whole = rows % LANES != 0
        if not whole:
            multiply(c, me, True)

        def step(j, _):
            arrived(c, j)
            if c + 1 < chunks:
                @pl.when(j == max(1, tensor_n - 2))
                def _():
                    ready(c + 1)
                    prepare(c + 1)
                    send(c + 1)

            if not whole:
                both(c, j)
            return 0

        lax.fori_loop(1, tensor_n, step, 0)
        if whole:
            multiply_all(c)
        each(1, tensor_n, lambda d: square_copy(c, around(d), around(d), d).wait_recv())
        finish(c)

    ready(0)
    prepare(0)
    send(0)
    for c in range(chunks):
        if c == 0:
            load_w.wait()
        compute(c)
        store_out(c).start()

        @pl.when(sec == 0)
        def _():
            handoff(c).start()

        @pl.when(sec == 1)
        def _():
            each(1, tensor_n, lambda d: part_copy(c, me, around(d), d).start())

    @pl.when(sec == 1)
    def _():
        segment = lax.broadcasted_iota(jnp.int32, (SEGS, LANES), 0)
        for m in range(micros):
            losses = jnp.zeros((SEGS, LANES), jnp.float32)
            counts = jnp.zeros((SEGS, LANES), jnp.float32)
            for h in range(per_micro):
                c = m * per_micro + h
                each(
                    1,
                    tensor_n,
                    lambda d: part_copy(c, around(d), around(d), d).wait_recv(),
                )
                cut = slice(h * LANES, (h + 1) * LANES)
                inv_root = lax.rsqrt(over_tensor(parts, c, 0) / width + epsilon)
                scores = over_tensor(parts, c, 8) * inv_root
                weight = mask_ref[m : m + 1, cut].astype(jnp.float32)
                off = scores - (labels_ref[m : m + 1, cut].astype(jnp.float32) - 1.0)
                member = seg_ref[m : m + 1, cut] == segment
                losses += jnp.where(member, weight * off * off, 0.0)
                counts += jnp.where(member, weight, 0.0)
            lc[dp, m * SEGS : (m + 1) * SEGS, :] = losses
            lc[dp, (micros + m) * SEGS : (micros + m + 1) * SEGS, :] = counts
        each(1, group, lambda k: loss_copy(dp, k).start())
        each(1, dp_n, lambda k: loss_copy(lax.rem(dp + k, dp_n), k).wait_recv())

    @pl.when(sec == 0)
    def _():
        each(0, dp_n, lambda k: loss_copy(lax.rem(dp + k, dp_n), 1 + k).wait_recv())

    total = lc[0]
    for k in range(1, dp_n):
        total = total + lc[k]
    total = jnp.sum(total, axis=1, keepdims=True)
    half = micros * SEGS
    loss = total[:half] / jnp.maximum(total[half:], 1.0)
    loss_ref[...] = jnp.broadcast_to(loss, loss_ref.shape)

    for c in range(chunks):
        sent(c)
        store_out(c).wait()

    @pl.when(sec == 0)
    def _():
        for c in range(chunks):
            handoff(c).wait_send()

    @pl.when(sec == 1)
    def _():
        for c in range(chunks):
            each(1, tensor_n, lambda d: part_copy(c, me, around(d), d).wait_send())
        each(1, group, lambda k: loss_copy(dp, k).wait_send())


def body(
    tensor_n,
    dp_n,
    tokens_in,
    section_proj,
    section_gain,
    final_gain,
    score_weight,
    labels,
    loss_mask,
    segment_ids,
):
    micros, rows, tokens = tokens_in.shape
    width = section_proj.shape[2]
    chunks = micros * (tokens // LANES)
    cols = jnp.stack(
        [
            section_gain[0].astype(jnp.float32),
            final_gain.astype(jnp.float32) * score_weight.astype(jnp.float32),
        ],
        axis=1,
    )
    dma = pltpu.SemaphoreType.DMA
    vmem = pl.BlockSpec(memory_space=pltpu.VMEM)
    hbm = pl.BlockSpec(memory_space=pl.ANY)
    out, loss = pl.pallas_call(
        functools.partial(kernel, tensor_n, dp_n, micros, width, rows),
        out_shape=(
            jax.ShapeDtypeStruct((micros, rows, tokens), jnp.bfloat16),
            jax.ShapeDtypeStruct((micros * SEGS, LANES), jnp.float32),
        ),
        in_specs=[hbm, hbm, vmem, vmem, vmem, vmem],
        out_specs=(hbm, vmem),
        scratch_shapes=[
            pltpu.VMEM((rows, width), jnp.bfloat16),
            pltpu.VMEM((chunks, rows, LANES), jnp.bfloat16),
            pltpu.VMEM((chunks, width, LANES), jnp.bfloat16),
            pltpu.VMEM((chunks, tensor_n, 8, LANES), jnp.float32),
            pltpu.VMEM((chunks, rows, LANES), jnp.bfloat16),
            pltpu.VMEM((rows, LANES), jnp.float32),
            pltpu.VMEM((chunks, tensor_n, 16, LANES), jnp.float32),
            pltpu.VMEM((dp_n, 2 * micros * SEGS, LANES), jnp.float32),
            dma,
            dma((chunks,)),
            dma((chunks,)),
            dma((chunks, tensor_n + 1)),
            dma((chunks, tensor_n)),
            dma((chunks, tensor_n)),
            dma((chunks, tensor_n)),
            dma((chunks,)),
            dma((chunks,)),
            dma((chunks, tensor_n)),
            dma((chunks, tensor_n)),
            dma((2 * dp_n,)),
            dma((dp_n,)),
        ],
        compiler_params=pltpu.CompilerParams(
            collective_id=0, has_side_effects=True, vmem_limit_bytes=56 * 2**20
        ),
        cost_estimate=pl.CostEstimate(
            flops=2 * rows * width * micros * tokens,
            bytes_accessed=2 * rows * width,
            transcendentals=0,
        ),
        name="relay",
    )(tokens_in, section_proj[0], cols, labels, loss_mask, segment_ids)
    return out[None], loss[:, 0].reshape(micros, SEGS)


def solution(mesh):
    in_specs = (
        P(None, "tensor", "dp"),
        P("section", "tensor", None),
        P("section", "tensor"),
        P("tensor"),
        P("tensor"),
        P(None, "dp"),
        P(None, "dp"),
        P(None, "dp"),
    )
    out_specs = (P("section", None, "tensor", "dp"), P())
    return jax.shard_map(
        functools.partial(body, mesh.shape["tensor"], mesh.shape["dp"]),
        mesh=mesh,
        in_specs=in_specs,
        out_specs=out_specs,
        check_vma=False,
    )
```

```python
import functools

import jax
import jax.numpy as jnp
from jax import lax
from jax.experimental import pallas as pl
from jax.experimental.pallas import tpu as pltpu
from jax.sharding import PartitionSpec as P

SEGS = 16
LANES = 128
epsilon = 1e-05
MESH = pl.DeviceIdType.MESH


def each(low, high, step):
    if high - low <= 8:
        for i in range(low, high):
            step(i)
    else:
        lax.fori_loop(low, high, lambda i, _: (step(i), 0)[1], 0)


def each_if(low, high, step):
    lax.fori_loop(low, high, lambda i, _: (step(i), 0)[1], 0)


def row_tile(rows):
    return next(t for t in range(256, 0, -16) if rows % t == 0)


def kernel(
    tensor_n,
    dp_n,
    micros,
    width,
    rows,
    tok_ref,
    w_ref,
    cols_ref,
    labels_ref,
    mask_ref,
    seg_ref,
    out_ref,
    loss_ref,
    w,
    x,
    g,
    sq,
    o,
    acc,
    own_gain,
    other_gain,
    relay,
    parts,
    lc,
    w_sem,
    tok_sem,
    out_sem,
    g_send,
    g_recv,
    q_send,
    q_recv,
    x_send,
    x_recv,
    p_send,
    p_recv,
    l_send,
    l_recv,
    r_send,
    r_recv,
    c_send,
    gain_send,
    gain_recv,
):
    chunks = x.shape[0]
    per_micro = chunks // micros
    tile = row_tile(rows)
    tiles = rows // tile
    band_rows = rows // 2 if rows % 32 == 0 else rows
    sec = lax.axis_index("section")
    dp = lax.axis_index("dp")
    me = lax.axis_index("tensor")
    group = 2 * dp_n
    place = sec * dp_n + dp

    def around(d):
        return lax.rem(me + d, tensor_n)

    def cousin(k):
        there = lax.rem(place + k, group)
        return {"section": there // dp_n, "dp": lax.rem(there, dp_n)}

    barrier = pltpu.get_barrier_semaphore()
    each(
        1,
        tensor_n,
        lambda d: pl.semaphore_signal(
            barrier, inc=1, device_id={"tensor": around(d)}, device_id_type=MESH
        ),
    )
    each(
        1,
        group,
        lambda k: pl.semaphore_signal(
            barrier, inc=1, device_id=cousin(k), device_id_type=MESH
        ),
    )

    load_w = pltpu.make_async_copy(w_ref, w, w_sem)

    def load_tok(c, to):
        return pltpu.make_async_copy(
            tok_ref.at[c // per_micro, :, pl.ds((c % per_micro) * LANES, LANES)],
            to.at[c],
            tok_sem.at[c],
        )

    gain_copy = pltpu.make_async_remote_copy(
        src_ref=own_gain,
        dst_ref=other_gain,
        send_sem=gain_send,
        recv_sem=gain_recv,
        device_id={"section": 1 - sec},
        device_id_type=MESH,
    )

    def store_out(c):
        return pltpu.make_async_copy(
            o.at[c],
            out_ref.at[c // per_micro, :, pl.ds((c % per_micro) * LANES, LANES)],
            out_sem.at[c],
        )

    def block(c, owner):
        return g.at[c, pl.ds(pl.multiple_of(owner * rows, 16), rows), :]

    def hop(c, owner, by, slot):
        return pltpu.make_async_remote_copy(
            src_ref=block(c, owner),
            dst_ref=block(c, owner),
            send_sem=g_send.at[c, slot],
            recv_sem=g_recv.at[c, owner],
            device_id={"tensor": lax.rem(me + by + tensor_n, tensor_n)},
            device_id_type=MESH,
        )

    def square_copy(c, owner, peer, d):
        return pltpu.make_async_remote_copy(
            src_ref=sq.at[c, owner],
            dst_ref=sq.at[c, owner],
            send_sem=q_send.at[c, d],
            recv_sem=q_recv.at[c, owner],
            device_id={"tensor": peer},
            device_id_type=MESH,
        )

    def part_copy(c, owner, peer, d):
        return pltpu.make_async_remote_copy(
            src_ref=parts.at[c, owner],
            dst_ref=parts.at[c, owner],
            send_sem=p_send.at[c, d],
            recv_sem=p_recv.at[c, owner],
            device_id={"tensor": peer},
            device_id_type=MESH,
        )

    def handoff(c):
        return pltpu.make_async_remote_copy(
            src_ref=o.at[c],
            dst_ref=x.at[c],
            send_sem=x_send.at[c],
            recv_sem=x_recv.at[c],
            device_id={"section": 1 - sec},
            device_id_type=MESH,
        )

    def loss_copy(owner, k):
        return pltpu.make_async_remote_copy(
            src_ref=lc.at[owner],
            dst_ref=lc.at[owner],
            send_sem=l_send.at[k],
            recv_sem=l_recv.at[owner],
            device_id=cousin(k),
            device_id_type=MESH,
        )

    @pl.when(sec == 0)
    def _():
        for c in range(chunks):
            load_tok(c, x).start()

    @pl.when(sec == 1)
    def _():
        load_tok(1, o).start()

    load_w.start()

    def spread(i, _):
        at = pl.ds(pl.multiple_of(i * tile, 16), tile)
        own_gain[at, :] = jnp.broadcast_to(cols_ref[at, 0:1], (tile, LANES)).astype(
            jnp.bfloat16
        )
        return 0

    lax.fori_loop(0, tiles, spread, 0)
    pl.semaphore_wait(barrier, tensor_n - 1 + group - 1)
    gain_copy.start()

    def ready(c):
        @pl.when(sec == 0)
        def _():
            load_tok(c, x).wait()

        @pl.when(sec == 1)
        def _():
            handoff(c).wait_recv()

    def folded(v):
        return jnp.sum(v.reshape(v.shape[0] // 8, 8, LANES), axis=0)

    def prepare(c):
        def step(i, total):
            at = pl.multiple_of(i * tile, 16)
            v = x[c, pl.ds(at, tile), :].astype(jnp.float32)
            gain = cols_ref[pl.ds(at, tile), 0:1]
            g[c, pl.ds(pl.multiple_of(me * rows + at, 16), tile), :] = (v * gain).astype(
                jnp.bfloat16
            )
            return total + folded(v * v)

        sq[c, me] = lax.fori_loop(0, tiles, step, jnp.zeros((8, LANES), jnp.float32))

    has_right = me + 1 < tensor_n
    has_left = me > 0

    def lent(owner, by, slot):
        at = relay.at[pl.ds(pl.multiple_of(owner * rows, 16), rows), :]
        return pltpu.make_async_remote_copy(
            src_ref=at,
            dst_ref=at,
            send_sem=r_send.at[slot],
            recv_sem=r_recv.at[owner],
            device_id={"tensor": lax.rem(me + by + tensor_n, tensor_n)},
            device_id_type=MESH,
        )

    def cross(c, owner):
        return pltpu.make_async_remote_copy(
            src_ref=relay.at[pl.ds(pl.multiple_of(owner * rows, 16), rows), :],
            dst_ref=block(c, owner),
            send_sem=c_send.at[owner],
            recv_sem=g_recv.at[c, owner],
            device_id={"section": 1 - sec},
            device_id_type=MESH,
        )

    def start_squares(c):
        each(1, tensor_n, lambda d: square_copy(c, me, around(d), d).start())

    def start_hops(copy):
        @pl.when(has_right)
        def _():
            copy(me, 1, me).start()

        @pl.when(has_left)
        def _():
            copy(me, -1, tensor_n).start()

    def wait_hops(copy):
        @pl.when(has_right)
        def _():
            each_if(0, me + 1, lambda s: copy(s, 1, s).wait_send())

        @pl.when(has_left)
        def _():
            copy(me, -1, tensor_n).wait_send()
            each_if(me + 1, tensor_n, lambda s: copy(s, -1, s).wait_send())

    def hops(c):
        return lambda owner, by, slot: hop(c, owner, by, slot)

    def send(c):
        start_squares(c)
        start_hops(hops(c))

    def pass_on(copy, j, further=None):
        @pl.when(me - j >= 0)
        def _():
            owner = me - j
            copy(owner, 1, owner).wait_recv()

            @pl.when(has_right)
            def _():
                copy(owner, 1, owner).start()

            if further:
                further(owner)

        @pl.when(me + j < tensor_n)
        def _():
            owner = me + j
            copy(owner, -1, owner).wait_recv()

            @pl.when(has_left)
            def _():
                copy(owner, -1, owner).start()

            if further:
                further(owner)

    def arrived(c, j):
        pass_on(hops(c), j)

    def crossed(c, j):
        @pl.when(me - j >= 0)
        def _():
            cross(c, me - j).wait_recv()

        @pl.when(me + j < tensor_n)
        def _():
            cross(c, me + j).wait_recv()

    def lend(c):
        gain_copy.wait_recv()

        def step(i, _):
            at = pl.multiple_of(i * tile, 16)
            v = o[c, pl.ds(at, tile), :].astype(jnp.float32)
            gain = other_gain[pl.ds(at, tile), :].astype(jnp.float32)
            relay[pl.ds(pl.multiple_of(me * rows + at, 16), tile), :] = (v * gain).astype(
                jnp.bfloat16
            )
            return 0

        lax.fori_loop(0, tiles, step, 0)
        start_hops(lent)
        each_if(
            1,
            tensor_n,
            lambda j: pass_on(lent, j, lambda owner: cross(c, owner).start()),
        )

    def over_tensor(ref, c, low):
        total = ref[c, 0, low : low + 8, :]
        for t in range(1, tensor_n):
            total = total + ref[c, t, low : low + 8, :]
        return jnp.sum(total, axis=0, keepdims=True)

    def multiply(c, owner, first):
        at = pl.multiple_of(owner * rows, 16)
        held = g[c, pl.ds(at, rows), :]

        def step(i, _):
            band = pl.ds(pl.multiple_of(i * band_rows, 16), band_rows)
            product = jnp.dot(
                w[band, pl.ds(pl.multiple_of(owner * rows, LANES), rows)],
                held,
                preferred_element_type=jnp.float32,
            )
            acc[band, :] = product if first else acc[band, :] + product
            return 0

        lax.fori_loop(0, rows // band_rows, step, 0)

    def both(c, j):
        @pl.when(me - j >= 0)
        def _():
            multiply(c, me - j, False)

        @pl.when(me + j < tensor_n)
        def _():
            multiply(c, me + j, False)

    def multiply_all(c):
        def step(i, _):
            band = pl.ds(pl.multiple_of(i * tile, 16), tile)
            acc[band, :] = jnp.dot(
                w[band, :], g[c], preferred_element_type=jnp.float32
            )
            return 0

        lax.fori_loop(0, tiles, step, 0)

    def finish(c):
        q = lax.rsqrt(over_tensor(sq, c, 0) / width + epsilon)

        def step(i, totals):
            at = pl.multiple_of(i * tile, 16)
            mixed = q * acc[pl.ds(at, tile), :]
            v = x[c, pl.ds(at, tile), :].astype(jnp.float32)
            result = (v + mixed / (1.0 + jnp.exp(-mixed))).astype(jnp.bfloat16)
            o[c, pl.ds(at, tile), :] = result
            f = result.astype(jnp.float32)
            head = cols_ref[pl.ds(at, tile), 1:2]
            return totals[0] + folded(f * f), totals[1] + folded(f * head)

        zero = jnp.zeros((8, LANES), jnp.float32)
        squares, dots = lax.fori_loop(0, tiles, step, (zero, zero))
        parts[c, me, 0:8, :] = squares
        parts[c, me, 8:16, :] = dots

    def run(c, meet, then=None, late=None):
        whole = rows % LANES != 0
        if not whole:
            multiply(c, me, True)

        def step(j, _):
            meet(j)
            if then:
                pl.when(j == max(1, tensor_n - 2))(then)
            if not whole:
                both(c, j)
            return 0

        lax.fori_loop(1, tensor_n, step, 0)
        if whole:
            multiply_all(c)
        if late:
            late()
        each(1, tensor_n, lambda d: square_copy(c, around(d), around(d), d).wait_recv())
        finish(c)
        store_out(c).start()

    assert chunks == 4
    last = chunks - 1

    @pl.when(sec == 0)
    def _():
        ready(0)
        prepare(0)
        send(0)
        load_w.wait()

        def then0():
            ready(2)
            prepare(2)
            send(2)
            ready(1)
            prepare(1)
            start_squares(1)

        run(0, lambda j: arrived(0, j), then0)
        handoff(0).start()

        def meet1(j):
            arrived(2, j)
            crossed(1, j)

        def then1():
            ready(3)
            prepare(3)
            send(3)

        run(1, meet1, then1)
        handoff(1).start()
        run(2, lambda j: None, None, lambda: arrived(3, 1))
        handoff(2).start()
        run(3, lambda j: pl.when(j > 1)(lambda: arrived(3, j)))
        handoff(3).start()
        lend(last)
        for c in (0, 2, 3):
            wait_hops(hops(c))

    @pl.when(sec == 1)
    def _():
        load_tok(1, o).wait()
        lend(1)
        ready(0)
        prepare(0)
        send(0)
        load_w.wait()
        for c in range(chunks):

            def then(c=c + 1):
                ready(c)
                prepare(c)
                if c < last:
                    send(c)
                else:
                    start_squares(c)

            run(
                c,
                (lambda j: arrived(c, j)) if c < last else (lambda j: crossed(c, j)),
                then if c < last else None,
            )
            each(1, tensor_n, lambda d: part_copy(c, me, around(d), d).start())
        for c in (0, 1, 2):
            wait_hops(hops(c))

    @pl.when(sec == 1)
    def _():
        segment = lax.broadcasted_iota(jnp.int32, (SEGS, LANES), 0)
        for m in range(micros):
            losses = jnp.zeros((SEGS, LANES), jnp.float32)
            counts = jnp.zeros((SEGS, LANES), jnp.float32)
            for h in range(per_micro):
                c = m * per_micro + h
                each(
                    1,
                    tensor_n,
                    lambda d: part_copy(c, around(d), around(d), d).wait_recv(),
                )
                cut = slice(h * LANES, (h + 1) * LANES)
                inv_root = lax.rsqrt(over_tensor(parts, c, 0) / width + epsilon)
                scores = over_tensor(parts, c, 8) * inv_root
                weight = mask_ref[m : m + 1, cut].astype(jnp.float32)
                off = scores - (labels_ref[m : m + 1, cut].astype(jnp.float32) - 1.0)
                member = seg_ref[m : m + 1, cut] == segment
                losses += jnp.where(member, weight * off * off, 0.0)
                counts += jnp.where(member, weight, 0.0)
            lc[dp, m * SEGS : (m + 1) * SEGS, :] = losses
            lc[dp, (micros + m) * SEGS : (micros + m + 1) * SEGS, :] = counts
        each(1, group, lambda k: loss_copy(dp, k).start())
        each(1, dp_n, lambda k: loss_copy(lax.rem(dp + k, dp_n), k).wait_recv())

    @pl.when(sec == 0)
    def _():
        each(0, dp_n, lambda k: loss_copy(lax.rem(dp + k, dp_n), 1 + k).wait_recv())

    total = lc[0]
    for k in range(1, dp_n):
        total = total + lc[k]
    total = jnp.sum(total, axis=1, keepdims=True)
    half = micros * SEGS
    loss = total[:half] / jnp.maximum(total[half:], 1.0)
    loss_ref[...] = jnp.broadcast_to(loss, loss_ref.shape)

    for c in range(chunks):
        each(1, tensor_n, lambda d: square_copy(c, me, around(d), d).wait_send())
        store_out(c).wait()
    wait_hops(lent)
    each(1, tensor_n, lambda d: cross(1, around(d)).wait_send())
    gain_copy.wait_send()

    @pl.when(sec == 0)
    def _():
        for c in range(chunks):
            handoff(c).wait_send()

    @pl.when(sec == 1)
    def _():
        for c in range(chunks):
            each(1, tensor_n, lambda d: part_copy(c, me, around(d), d).wait_send())
        each(1, group, lambda k: loss_copy(dp, k).wait_send())


def body(
    tensor_n,
    dp_n,
    tokens_in,
    section_proj,
    section_gain,
    final_gain,
    score_weight,
    labels,
    loss_mask,
    segment_ids,
):
    micros, rows, tokens = tokens_in.shape
    width = section_proj.shape[2]
    chunks = micros * (tokens // LANES)
    cols = jnp.stack(
        [
            section_gain[0].astype(jnp.float32),
            final_gain.astype(jnp.float32) * score_weight.astype(jnp.float32),
        ],
        axis=1,
    )
    dma = pltpu.SemaphoreType.DMA
    vmem = pl.BlockSpec(memory_space=pltpu.VMEM)
    hbm = pl.BlockSpec(memory_space=pl.ANY)
    out, loss = pl.pallas_call(
        functools.partial(kernel, tensor_n, dp_n, micros, width, rows),
        out_shape=(
            jax.ShapeDtypeStruct((micros, rows, tokens), jnp.bfloat16),
            jax.ShapeDtypeStruct((micros * SEGS, LANES), jnp.float32),
        ),
        in_specs=[hbm, hbm, vmem, vmem, vmem, vmem],
        out_specs=(hbm, vmem),
        scratch_shapes=[
            pltpu.VMEM((rows, width), jnp.bfloat16),
            pltpu.VMEM((chunks, rows, LANES), jnp.bfloat16),
            pltpu.VMEM((chunks, width, LANES), jnp.bfloat16),
            pltpu.VMEM((chunks, tensor_n, 8, LANES), jnp.float32),
            pltpu.VMEM((chunks, rows, LANES), jnp.bfloat16),
            pltpu.VMEM((rows, LANES), jnp.float32),
            pltpu.VMEM((rows, LANES), jnp.bfloat16),
            pltpu.VMEM((rows, LANES), jnp.bfloat16),
            pltpu.VMEM((width, LANES), jnp.bfloat16),
            pltpu.VMEM((chunks, tensor_n, 16, LANES), jnp.float32),
            pltpu.VMEM((dp_n, 2 * micros * SEGS, LANES), jnp.float32),
            dma,
            dma((chunks,)),
            dma((chunks,)),
            dma((chunks, tensor_n + 1)),
            dma((chunks, tensor_n)),
            dma((chunks, tensor_n)),
            dma((chunks, tensor_n)),
            dma((chunks,)),
            dma((chunks,)),
            dma((chunks, tensor_n)),
            dma((chunks, tensor_n)),
            dma((2 * dp_n,)),
            dma((dp_n,)),
            dma((tensor_n + 1,)),
            dma((tensor_n,)),
            dma((tensor_n,)),
            dma,
            dma,
        ],
        compiler_params=pltpu.CompilerParams(
            collective_id=0, has_side_effects=True, vmem_limit_bytes=56 * 2**20
        ),
        cost_estimate=pl.CostEstimate(
            flops=2 * rows * width * micros * tokens,
            bytes_accessed=2 * rows * width,
            transcendentals=0,
        ),
        name="relay",
    )(tokens_in, section_proj[0], cols, labels, loss_mask, segment_ids)
    return out[None], loss[:, 0].reshape(micros, SEGS)


def solution(mesh):
    in_specs = (
        P(None, "tensor", "dp"),
        P("section", "tensor", None),
        P("section", "tensor"),
        P("tensor"),
        P("tensor"),
        P(None, "dp"),
        P(None, "dp"),
        P(None, "dp"),
    )
    out_specs = (P("section", None, "tensor", "dp"), P())
    return jax.shard_map(
        functools.partial(body, mesh.shape["tensor"], mesh.shape["dp"]),
        mesh=mesh,
        in_specs=in_specs,
        out_specs=out_specs,
        check_vma=False,
    )
```

```python
import functools

import jax
import jax.numpy as jnp
from jax import lax
from jax.experimental import pallas as pl
from jax.experimental.pallas import tpu as pltpu
from jax.sharding import PartitionSpec as P

SEGS = 16
LANES = 128
epsilon = 1e-05
MESH = pl.DeviceIdType.MESH


def each(low, high, step):
    if high - low <= 8:
        for i in range(low, high):
            step(i)
    else:
        lax.fori_loop(low, high, lambda i, _: (step(i), 0)[1], 0)


def each_if(low, high, step):
    lax.fori_loop(low, high, lambda i, _: (step(i), 0)[1], 0)


def row_tile(rows):
    return next(t for t in range(256, 0, -16) if rows % t == 0)


def kernel(
    tensor_n,
    dp_n,
    micros,
    width,
    rows,
    tok_ref,
    w_ref,
    cols_ref,
    labels_ref,
    mask_ref,
    seg_ref,
    out_ref,
    loss_ref,
    w,
    x,
    g,
    sq,
    o,
    acc,
    own_gain,
    other_gain,
    relay,
    parts,
    lc,
    w_sem,
    tok_sem,
    out_sem,
    g_send,
    g_recv,
    q_send,
    q_recv,
    x_send,
    x_recv,
    p_send,
    p_recv,
    l_send,
    l_recv,
    r_send,
    r_recv,
    c_send,
    gain_send,
    gain_recv,
):
    chunks = x.shape[0]
    per_micro = chunks // micros
    tile = row_tile(rows)
    tiles = rows // tile
    band_rows = rows // 2 if rows % 32 == 0 else rows
    sec = lax.axis_index("section")
    dp = lax.axis_index("dp")
    me = lax.axis_index("tensor")
    group = 2 * dp_n
    place = sec * dp_n + dp

    def around(d):
        return lax.rem(me + d, tensor_n)

    def cousin(k):
        there = lax.rem(place + k, group)
        return {"section": there // dp_n, "dp": lax.rem(there, dp_n)}

    barrier = pltpu.get_barrier_semaphore()
    each(
        1,
        tensor_n,
        lambda d: pl.semaphore_signal(
            barrier, inc=1, device_id={"tensor": around(d)}, device_id_type=MESH
        ),
    )
    each(
        1,
        group,
        lambda k: pl.semaphore_signal(
            barrier, inc=1, device_id=cousin(k), device_id_type=MESH
        ),
    )

    load_w = pltpu.make_async_copy(w_ref, w, w_sem)

    def load_tok(c, to):
        return pltpu.make_async_copy(
            tok_ref.at[c // per_micro, :, pl.ds((c % per_micro) * LANES, LANES)],
            to.at[c],
            tok_sem.at[c],
        )

    gain_copy = pltpu.make_async_remote_copy(
        src_ref=own_gain,
        dst_ref=other_gain,
        send_sem=gain_send,
        recv_sem=gain_recv,
        device_id={"section": 1 - sec},
        device_id_type=MESH,
    )

    def store_out(c):
        return pltpu.make_async_copy(
            o.at[c],
            out_ref.at[c // per_micro, :, pl.ds((c % per_micro) * LANES, LANES)],
            out_sem.at[c],
        )

    def block(c, owner):
        return g.at[c, pl.ds(pl.multiple_of(owner * rows, 16), rows), :]

    def hop(c, owner, by, slot):
        return pltpu.make_async_remote_copy(
            src_ref=block(c, owner),
            dst_ref=block(c, owner),
            send_sem=g_send.at[c, slot],
            recv_sem=g_recv.at[c, owner],
            device_id={"tensor": lax.rem(me + by + tensor_n, tensor_n)},
            device_id_type=MESH,
        )

    def square_copy(c, owner, peer, d):
        return pltpu.make_async_remote_copy(
            src_ref=sq.at[c, owner],
            dst_ref=sq.at[c, owner],
            send_sem=q_send.at[c, d],
            recv_sem=q_recv.at[c, owner],
            device_id={"tensor": peer},
            device_id_type=MESH,
        )

    def part_copy(c, owner, peer, d):
        return pltpu.make_async_remote_copy(
            src_ref=parts.at[c, owner],
            dst_ref=parts.at[c, owner],
            send_sem=p_send.at[c, d],
            recv_sem=p_recv.at[c, owner],
            device_id={"tensor": peer},
            device_id_type=MESH,
        )

    def handoff(c, i):
        band = pl.ds(pl.multiple_of(i * tile, 16), tile)
        return pltpu.make_async_remote_copy(
            src_ref=o.at[c, band, :],
            dst_ref=x.at[c, band, :],
            send_sem=x_send.at[c, i],
            recv_sem=x_recv.at[c, i],
            device_id={"section": 1 - sec},
            device_id_type=MESH,
        )

    def loss_copy(owner, k):
        return pltpu.make_async_remote_copy(
            src_ref=lc.at[owner],
            dst_ref=lc.at[owner],
            send_sem=l_send.at[k],
            recv_sem=l_recv.at[owner],
            device_id=cousin(k),
            device_id_type=MESH,
        )

    @pl.when(sec == 0)
    def _():
        for c in range(chunks):
            load_tok(c, x).start()

    @pl.when(sec == 1)
    def _():
        load_tok(1, o).start()

    load_w.start()

    def spread(i, _):
        at = pl.ds(pl.multiple_of(i * tile, 16), tile)
        own_gain[at, :] = jnp.broadcast_to(cols_ref[at, 0:1], (tile, LANES)).astype(
            jnp.bfloat16
        )
        return 0

    lax.fori_loop(0, tiles, spread, 0)
    pl.semaphore_wait(barrier, tensor_n - 1 + group - 1)
    gain_copy.start()

    def folded(v):
        return jnp.sum(v.reshape(v.shape[0] // 8, 8, LANES), axis=0)

    def prepare(c, handed):
        if not handed:
            load_tok(c, x).wait()

        def step(i, total):
            if handed:
                handoff(c, i).wait_recv()
            at = pl.multiple_of(i * tile, 16)
            v = x[c, pl.ds(at, tile), :].astype(jnp.float32)
            gain = cols_ref[pl.ds(at, tile), 0:1]
            g[c, pl.ds(pl.multiple_of(me * rows + at, 16), tile), :] = (v * gain).astype(
                jnp.bfloat16
            )
            return total + folded(v * v)

        sq[c, me] = lax.fori_loop(0, tiles, step, jnp.zeros((8, LANES), jnp.float32))

    has_right = me + 1 < tensor_n
    has_left = me > 0

    def lent(owner, by, slot):
        at = relay.at[pl.ds(pl.multiple_of(owner * rows, 16), rows), :]
        return pltpu.make_async_remote_copy(
            src_ref=at,
            dst_ref=at,
            send_sem=r_send.at[slot],
            recv_sem=r_recv.at[owner],
            device_id={"tensor": lax.rem(me + by + tensor_n, tensor_n)},
            device_id_type=MESH,
        )

    def cross(c, owner):
        return pltpu.make_async_remote_copy(
            src_ref=relay.at[pl.ds(pl.multiple_of(owner * rows, 16), rows), :],
            dst_ref=block(c, owner),
            send_sem=c_send.at[owner],
            recv_sem=g_recv.at[c, owner],
            device_id={"section": 1 - sec},
            device_id_type=MESH,
        )

    def start_squares(c):
        each(1, tensor_n, lambda d: square_copy(c, me, around(d), d).start())

    def start_hops(copy):
        @pl.when(has_right)
        def _():
            copy(me, 1, me).start()

        @pl.when(has_left)
        def _():
            copy(me, -1, tensor_n).start()

    def wait_hops(copy):
        @pl.when(has_right)
        def _():
            each_if(0, me + 1, lambda s: copy(s, 1, s).wait_send())

        @pl.when(has_left)
        def _():
            copy(me, -1, tensor_n).wait_send()
            each_if(me + 1, tensor_n, lambda s: copy(s, -1, s).wait_send())

    def hops(c):
        return lambda owner, by, slot: hop(c, owner, by, slot)

    def send(c):
        start_squares(c)
        start_hops(hops(c))

    def pass_on(copy, j, further=None):
        @pl.when(me - j >= 0)
        def _():
            owner = me - j
            copy(owner, 1, owner).wait_recv()

            @pl.when(has_right)
            def _():
                copy(owner, 1, owner).start()

            if further:
                further(owner)

        @pl.when(me + j < tensor_n)
        def _():
            owner = me + j
            copy(owner, -1, owner).wait_recv()

            @pl.when(has_left)
            def _():
                copy(owner, -1, owner).start()

            if further:
                further(owner)

    def arrived(c, j):
        pass_on(hops(c), j)

    def crossed(c, j):
        @pl.when(me - j >= 0)
        def _():
            cross(c, me - j).wait_recv()

        @pl.when(me + j < tensor_n)
        def _():
            cross(c, me + j).wait_recv()

    def lend(c):
        gain_copy.wait_recv()

        def step(i, _):
            at = pl.multiple_of(i * tile, 16)
            v = o[c, pl.ds(at, tile), :].astype(jnp.float32)
            gain = other_gain[pl.ds(at, tile), :].astype(jnp.float32)
            relay[pl.ds(pl.multiple_of(me * rows + at, 16), tile), :] = (v * gain).astype(
                jnp.bfloat16
            )
            return 0

        lax.fori_loop(0, tiles, step, 0)
        start_hops(lent)
        each_if(
            1,
            tensor_n,
            lambda j: pass_on(lent, j, lambda owner: cross(c, owner).start()),
        )

    def over_tensor(ref, c, low):
        total = ref[c, 0, low : low + 8, :]
        for t in range(1, tensor_n):
            total = total + ref[c, t, low : low + 8, :]
        return jnp.sum(total, axis=0, keepdims=True)

    def multiply(c, owner, first):
        at = pl.multiple_of(owner * rows, 16)
        held = g[c, pl.ds(at, rows), :]

        def step(i, _):
            band = pl.ds(pl.multiple_of(i * band_rows, 16), band_rows)
            product = jnp.dot(
                w[band, pl.ds(pl.multiple_of(owner * rows, LANES), rows)],
                held,
                preferred_element_type=jnp.float32,
            )
            acc[c % 2, band, :] = product if first else acc[c % 2, band, :] + product
            return 0

        lax.fori_loop(0, rows // band_rows, step, 0)

    def both(c, j):
        @pl.when(me - j >= 0)
        def _():
            multiply(c, me - j, False)

        @pl.when(me + j < tensor_n)
        def _():
            multiply(c, me + j, False)

    def multiply_all(c):
        def step(i, _):
            band = pl.ds(pl.multiple_of(i * tile, 16), tile)
            acc[c % 2, band, :] = jnp.dot(
                w[band, :], g[c], preferred_element_type=jnp.float32
            )
            return 0

        lax.fori_loop(0, tiles, step, 0)

    def finish(c, hand):
        each(1, tensor_n, lambda d: square_copy(c, around(d), around(d), d).wait_recv())
        q = lax.rsqrt(over_tensor(sq, c, 0) / width + epsilon)

        def step(i, totals):
            at = pl.multiple_of(i * tile, 16)
            mixed = q * acc[c % 2, pl.ds(at, tile), :]
            v = x[c, pl.ds(at, tile), :].astype(jnp.float32)
            result = (v + mixed / (1.0 + jnp.exp(-mixed))).astype(jnp.bfloat16)
            o[c, pl.ds(at, tile), :] = result
            if hand:
                handoff(c, i).start()
            f = result.astype(jnp.float32)
            head = cols_ref[pl.ds(at, tile), 1:2]
            return totals[0] + folded(f * f), totals[1] + folded(f * head)

        zero = jnp.zeros((8, LANES), jnp.float32)
        squares, dots = lax.fori_loop(0, tiles, step, (zero, zero))
        parts[c, me, 0:8, :] = squares
        parts[c, me, 8:16, :] = dots
        store_out(c).start()
        if not hand:
            each(1, tensor_n, lambda d: part_copy(c, me, around(d), d).start())

    whole = rows % LANES != 0

    def begin(c):
        if not whole:
            multiply(c, me, True)

    def add(c, j):
        if not whole:
            both(c, j)

    def close(c, hand):
        if whole:
            multiply_all(c)
        finish(c, hand)

    turn = max(1, tensor_n - 2)

    def run(c, hand, meet, then=None):
        begin(c)

        def step(j, _):
            meet(j)
            if then:
                pl.when(j == turn)(then)
            add(c, j)
            return 0

        lax.fori_loop(1, tensor_n, step, 0)
        close(c, hand)

    assert chunks == 4
    last = chunks - 1

    @pl.when(sec == 0)
    def _():
        prepare(0, False)
        send(0)
        load_w.wait()

        def then0():
            prepare(2, False)
            send(2)
            prepare(1, False)
            start_squares(1)

        run(0, True, lambda j: arrived(0, j), then0)

        def meet1(j):
            pl.when(j == 1)(lambda: arrived(2, 1))
            crossed(1, j)

        run(1, True, meet1)

        def then2():
            prepare(3, False)
            send(3)

        run(2, True, lambda j: pl.when(j > 1)(lambda: arrived(2, j)), then2)
        run(3, True, lambda j: arrived(3, j))
        lend(last)
        for c in (0, 2, 3):
            wait_hops(hops(c))

    @pl.when(sec == 1)
    def _():
        load_tok(1, o).wait()
        lend(1)
        prepare(0, True)
        send(0)
        load_w.wait()
        for c in range(last - 1):

            def then(c=c + 1):
                prepare(c, True)
                send(c)

            run(c, False, lambda j: arrived(c, j), then)

        c = last - 1
        begin(c)

        def step(j, _):
            arrived(c, j)
            add(c, j)

            @pl.when(j == turn)
            def _():
                prepare(last, True)
                start_squares(last)
                begin(last)

            @pl.when(j > turn)
            def _():
                def catch_up(k, _):
                    crossed(last, k)
                    add(last, k)
                    return 0

                lax.fori_loop(1, turn + 1, catch_up, 0)

            return 0

        lax.fori_loop(1, tensor_n, step, 0)
        close(c, False)
        crossed(last, tensor_n - 1)
        add(last, tensor_n - 1)
        close(last, False)
        for c in (0, 1, 2):
            wait_hops(hops(c))

    @pl.when(sec == 1)
    def _():
        segment = lax.broadcasted_iota(jnp.int32, (SEGS, LANES), 0)
        for m in range(micros):
            losses = jnp.zeros((SEGS, LANES), jnp.float32)
            counts = jnp.zeros((SEGS, LANES), jnp.float32)
            for h in range(per_micro):
                c = m * per_micro + h
                each(
                    1,
                    tensor_n,
                    lambda d: part_copy(c, around(d), around(d), d).wait_recv(),
                )
                cut = slice(h * LANES, (h + 1) * LANES)
                inv_root = lax.rsqrt(over_tensor(parts, c, 0) / width + epsilon)
                scores = over_tensor(parts, c, 8) * inv_root
                weight = mask_ref[m : m + 1, cut].astype(jnp.float32)
                off = scores - (labels_ref[m : m + 1, cut].astype(jnp.float32) - 1.0)
                member = seg_ref[m : m + 1, cut] == segment
                losses += jnp.where(member, weight * off * off, 0.0)
                counts += jnp.where(member, weight, 0.0)
            lc[dp, m * SEGS : (m + 1) * SEGS, :] = losses
            lc[dp, (micros + m) * SEGS : (micros + m + 1) * SEGS, :] = counts
        each(1, group, lambda k: loss_copy(dp, k).start())
        each(1, dp_n, lambda k: loss_copy(lax.rem(dp + k, dp_n), k).wait_recv())

    @pl.when(sec == 0)
    def _():
        each(0, dp_n, lambda k: loss_copy(lax.rem(dp + k, dp_n), 1 + k).wait_recv())

    total = lc[0]
    for k in range(1, dp_n):
        total = total + lc[k]
    total = jnp.sum(total, axis=1, keepdims=True)
    half = micros * SEGS
    loss = total[:half] / jnp.maximum(total[half:], 1.0)
    lane = lax.broadcasted_iota(jnp.int32, (SEGS, LANES), 1)
    diagonal = lane == lax.broadcasted_iota(jnp.int32, (SEGS, LANES), 0)
    for m in range(micros):
        column = jnp.broadcast_to(loss[m * SEGS : (m + 1) * SEGS], (SEGS, LANES))
        row = jnp.sum(jnp.where(diagonal, column, 0.0), axis=0, keepdims=True)
        loss_ref[m : m + 1, :] = row[:, :SEGS]

    for c in range(chunks):
        each(1, tensor_n, lambda d: square_copy(c, me, around(d), d).wait_send())
        store_out(c).wait()
    wait_hops(lent)
    each(1, tensor_n, lambda d: cross(1, around(d)).wait_send())
    gain_copy.wait_send()

    @pl.when(sec == 0)
    def _():
        for c in range(chunks):
            each(0, tiles, lambda i: handoff(c, i).wait_send())

    @pl.when(sec == 1)
    def _():
        for c in range(chunks):
            each(1, tensor_n, lambda d: part_copy(c, me, around(d), d).wait_send())
        each(1, group, lambda k: loss_copy(dp, k).wait_send())


def body(
    tensor_n,
    dp_n,
    tokens_in,
    section_proj,
    section_gain,
    final_gain,
    score_weight,
    labels,
    loss_mask,
    segment_ids,
):
    micros, rows, tokens = tokens_in.shape
    width = section_proj.shape[2]
    chunks = micros * (tokens // LANES)
    cols = jnp.stack(
        [
            section_gain[0].astype(jnp.float32),
            final_gain.astype(jnp.float32) * score_weight.astype(jnp.float32),
        ],
        axis=1,
    )
    dma = pltpu.SemaphoreType.DMA
    vmem = pl.BlockSpec(memory_space=pltpu.VMEM)
    hbm = pl.BlockSpec(memory_space=pl.ANY)
    out, loss = pl.pallas_call(
        functools.partial(kernel, tensor_n, dp_n, micros, width, rows),
        out_shape=(
            jax.ShapeDtypeStruct((micros, rows, tokens), jnp.bfloat16),
            jax.ShapeDtypeStruct((micros, SEGS), jnp.float32),
        ),
        in_specs=[hbm, hbm, vmem, vmem, vmem, vmem],
        out_specs=(hbm, vmem),
        scratch_shapes=[
            pltpu.VMEM((rows, width), jnp.bfloat16),
            pltpu.VMEM((chunks, rows, LANES), jnp.bfloat16),
            pltpu.VMEM((chunks, width, LANES), jnp.bfloat16),
            pltpu.VMEM((chunks, tensor_n, 8, LANES), jnp.float32),
            pltpu.VMEM((chunks, rows, LANES), jnp.bfloat16),
            pltpu.VMEM((2, rows, LANES), jnp.float32),
            pltpu.VMEM((rows, LANES), jnp.bfloat16),
            pltpu.VMEM((rows, LANES), jnp.bfloat16),
            pltpu.VMEM((width, LANES), jnp.bfloat16),
            pltpu.VMEM((chunks, tensor_n, 16, LANES), jnp.float32),
            pltpu.VMEM((dp_n, 2 * micros * SEGS, LANES), jnp.float32),
            dma,
            dma((chunks,)),
            dma((chunks,)),
            dma((chunks, tensor_n + 1)),
            dma((chunks, tensor_n)),
            dma((chunks, tensor_n)),
            dma((chunks, tensor_n)),
            dma((chunks, rows // row_tile(rows))),
            dma((chunks, rows // row_tile(rows))),
            dma((chunks, tensor_n)),
            dma((chunks, tensor_n)),
            dma((2 * dp_n,)),
            dma((dp_n,)),
            dma((tensor_n + 1,)),
            dma((tensor_n,)),
            dma((tensor_n,)),
            dma,
            dma,
        ],
        compiler_params=pltpu.CompilerParams(
            collective_id=0, has_side_effects=True, vmem_limit_bytes=56 * 2**20
        ),
        cost_estimate=pl.CostEstimate(
            flops=2 * rows * width * micros * tokens,
            bytes_accessed=2 * rows * width,
            transcendentals=0,
        ),
        name="relay",
    )(tokens_in, section_proj[0], cols, labels, loss_mask, segment_ids)
    return out[None], loss


def solution(mesh):
    in_specs = (
        P(None, "tensor", "dp"),
        P("section", "tensor", None),
        P("section", "tensor"),
        P("tensor"),
        P("tensor"),
        P(None, "dp"),
        P(None, "dp"),
        P(None, "dp"),
    )
    out_specs = (P("section", None, "tensor", "dp"), P())
    return jax.shard_map(
        functools.partial(body, mesh.shape["tensor"], mesh.shape["dp"]),
        mesh=mesh,
        in_specs=in_specs,
        out_specs=out_specs,
        check_vma=False,
    )
```

```python
import functools

import jax
import jax.numpy as jnp
from jax import lax
from jax.experimental import pallas as pl
from jax.experimental.pallas import tpu as pltpu
from jax.sharding import PartitionSpec as P

SEGS = 16
PIECES = 2
LANES = 128
epsilon = 1e-05
MESH = pl.DeviceIdType.MESH


def each(low, high, step):
    if high - low <= 8:
        for i in range(low, high):
            step(i)
    else:
        lax.fori_loop(low, high, lambda i, _: (step(i), 0)[1], 0)


def each_if(low, high, step):
    lax.fori_loop(low, high, lambda i, _: (step(i), 0)[1], 0)


def row_tile(rows):
    return next(t for t in range(256, 0, -16) if rows % t == 0)


def kernel(
    tensor_n,
    dp_n,
    micros,
    width,
    rows,
    tok_ref,
    w_ref,
    cols_ref,
    labels_ref,
    mask_ref,
    seg_ref,
    out_ref,
    loss_ref,
    w,
    x,
    g,
    sq,
    o,
    acc,
    own_gain,
    other_gain,
    relay,
    parts,
    lc,
    w_sem,
    tok_sem,
    out_sem,
    g_send,
    g_recv,
    q_send,
    q_recv,
    x_send,
    x_recv,
    p_send,
    p_recv,
    l_send,
    l_recv,
    r_send,
    r_recv,
    c_send,
    gain_send,
    gain_recv,
):
    chunks = x.shape[0]
    per_micro = chunks // micros
    tile = row_tile(rows)
    tiles = rows // tile
    band_rows = rows // 2 if rows % 32 == 0 else rows
    sec = lax.axis_index("section")
    dp = lax.axis_index("dp")
    me = lax.axis_index("tensor")
    group = 2 * dp_n
    place = sec * dp_n + dp

    def around(d):
        return lax.rem(me + d, tensor_n)

    def cousin(k):
        there = lax.rem(place + k, group)
        return {"section": there // dp_n, "dp": lax.rem(there, dp_n)}

    barrier = pltpu.get_barrier_semaphore()
    each(
        1,
        tensor_n,
        lambda d: pl.semaphore_signal(
            barrier, inc=1, device_id={"tensor": around(d)}, device_id_type=MESH
        ),
    )
    each(
        1,
        group,
        lambda k: pl.semaphore_signal(
            barrier, inc=1, device_id=cousin(k), device_id_type=MESH
        ),
    )

    load_w = pltpu.make_async_copy(w_ref, w, w_sem)

    def load_tok(c, to):
        return pltpu.make_async_copy(
            tok_ref.at[c // per_micro, :, pl.ds((c % per_micro) * LANES, LANES)],
            to.at[c],
            tok_sem.at[c],
        )

    gain_copy = pltpu.make_async_remote_copy(
        src_ref=own_gain,
        dst_ref=other_gain,
        send_sem=gain_send,
        recv_sem=gain_recv,
        device_id={"section": 1 - sec},
        device_id_type=MESH,
    )

    def store_out(c):
        return pltpu.make_async_copy(
            o.at[c],
            out_ref.at[c // per_micro, :, pl.ds((c % per_micro) * LANES, LANES)],
            out_sem.at[c],
        )

    def piece_of(owner, h):
        size = rows // PIECES
        return pl.ds(pl.multiple_of(owner * rows + h * size, 16), size)

    def block(c, owner, h):
        return g.at[c, piece_of(owner, h), :]

    def hop(c, owner, by, slot, h):
        return pltpu.make_async_remote_copy(
            src_ref=block(c, owner, h),
            dst_ref=block(c, owner, h),
            send_sem=g_send.at[c, slot, h],
            recv_sem=g_recv.at[c, owner, h],
            device_id={"tensor": lax.rem(me + by + tensor_n, tensor_n)},
            device_id_type=MESH,
        )

    def square_copy(c, owner, peer, d):
        return pltpu.make_async_remote_copy(
            src_ref=sq.at[c, owner],
            dst_ref=sq.at[c, owner],
            send_sem=q_send.at[c, d],
            recv_sem=q_recv.at[c, owner],
            device_id={"tensor": peer},
            device_id_type=MESH,
        )

    def part_copy(c, owner, peer, d):
        return pltpu.make_async_remote_copy(
            src_ref=parts.at[c, owner],
            dst_ref=parts.at[c, owner],
            send_sem=p_send.at[c, d],
            recv_sem=p_recv.at[c, owner],
            device_id={"tensor": peer},
            device_id_type=MESH,
        )

    def handoff(c, i):
        band = pl.ds(pl.multiple_of(i * tile, 16), tile)
        return pltpu.make_async_remote_copy(
            src_ref=o.at[c, band, :],
            dst_ref=x.at[c, band, :],
            send_sem=x_send.at[c, i],
            recv_sem=x_recv.at[c, i],
            device_id={"section": 1 - sec},
            device_id_type=MESH,
        )

    def loss_copy(owner, k):
        return pltpu.make_async_remote_copy(
            src_ref=lc.at[owner],
            dst_ref=lc.at[owner],
            send_sem=l_send.at[k],
            recv_sem=l_recv.at[owner],
            device_id=cousin(k),
            device_id_type=MESH,
        )

    @pl.when(sec == 0)
    def _():
        for c in range(chunks):
            load_tok(c, x).start()

    @pl.when(sec == 1)
    def _():
        load_tok(1, o).start()

    load_w.start()

    def spread(i, _):
        at = pl.ds(pl.multiple_of(i * tile, 16), tile)
        own_gain[at, :] = jnp.broadcast_to(cols_ref[at, 0:1], (tile, LANES)).astype(
            jnp.bfloat16
        )
        return 0

    lax.fori_loop(0, tiles, spread, 0)
    pl.semaphore_wait(barrier, tensor_n - 1 + group - 1)
    gain_copy.start()

    def folded(v):
        return jnp.sum(v.reshape(v.shape[0] // 8, 8, LANES), axis=0)

    def prepare(c, handed):
        if not handed:
            load_tok(c, x).wait()

        def step(i, total):
            if handed:
                handoff(c, i).wait_recv()
            at = pl.multiple_of(i * tile, 16)
            v = x[c, pl.ds(at, tile), :].astype(jnp.float32)
            gain = cols_ref[pl.ds(at, tile), 0:1]
            g[c, pl.ds(pl.multiple_of(me * rows + at, 16), tile), :] = (v * gain).astype(
                jnp.bfloat16
            )
            return total + folded(v * v)

        sq[c, me] = lax.fori_loop(0, tiles, step, jnp.zeros((8, LANES), jnp.float32))

    has_right = me + 1 < tensor_n
    has_left = me > 0

    def lent(owner, by, slot, h):
        at = relay.at[piece_of(owner, h), :]
        return pltpu.make_async_remote_copy(
            src_ref=at,
            dst_ref=at,
            send_sem=r_send.at[slot, h],
            recv_sem=r_recv.at[owner, h],
            device_id={"tensor": lax.rem(me + by + tensor_n, tensor_n)},
            device_id_type=MESH,
        )

    def cross(c, owner, h):
        return pltpu.make_async_remote_copy(
            src_ref=relay.at[piece_of(owner, h), :],
            dst_ref=block(c, owner, h),
            send_sem=c_send.at[owner, h],
            recv_sem=g_recv.at[c, owner, h],
            device_id={"section": 1 - sec},
            device_id_type=MESH,
        )

    def start_squares(c):
        each(1, tensor_n, lambda d: square_copy(c, me, around(d), d).start())

    def start_hops(copy):
        for h in range(PIECES):

            @pl.when(has_right)
            def _():
                copy(me, 1, me, h).start()

            @pl.when(has_left)
            def _():
                copy(me, -1, tensor_n, h).start()

    def wait_hops(copy):
        for h in range(PIECES):

            @pl.when(has_right)
            def _():
                each_if(0, me + 1, lambda s: copy(s, 1, s, h).wait_send())

            @pl.when(has_left)
            def _():
                copy(me, -1, tensor_n, h).wait_send()
                each_if(me + 1, tensor_n, lambda s: copy(s, -1, s, h).wait_send())

    def hops(c):
        return lambda owner, by, slot, h: hop(c, owner, by, slot, h)

    def send(c):
        start_squares(c)
        start_hops(hops(c))

    def pass_on(copy, j, further=None):
        for h in range(PIECES):

            @pl.when(me - j >= 0)
            def _():
                owner = me - j
                copy(owner, 1, owner, h).wait_recv()

                @pl.when(has_right)
                def _():
                    copy(owner, 1, owner, h).start()

                if further:
                    further(owner, h)

            @pl.when(me + j < tensor_n)
            def _():
                owner = me + j
                copy(owner, -1, owner, h).wait_recv()

                @pl.when(has_left)
                def _():
                    copy(owner, -1, owner, h).start()

                if further:
                    further(owner, h)

    def arrived(c, j):
        pass_on(hops(c), j)

    def crossed(c, j):
        for h in range(PIECES):

            @pl.when(me - j >= 0)
            def _():
                cross(c, me - j, h).wait_recv()

            @pl.when(me + j < tensor_n)
            def _():
                cross(c, me + j, h).wait_recv()

    def lend(c):
        gain_copy.wait_recv()

        def step(i, _):
            at = pl.multiple_of(i * tile, 16)
            v = o[c, pl.ds(at, tile), :].astype(jnp.float32)
            gain = other_gain[pl.ds(at, tile), :].astype(jnp.float32)
            relay[pl.ds(pl.multiple_of(me * rows + at, 16), tile), :] = (v * gain).astype(
                jnp.bfloat16
            )
            return 0

        lax.fori_loop(0, tiles, step, 0)
        start_hops(lent)
        each_if(
            1,
            tensor_n,
            lambda j: pass_on(lent, j, lambda owner, h: cross(c, owner, h).start()),
        )

    def over_tensor(ref, c, low):
        total = ref[c, 0, low : low + 8, :]
        for t in range(1, tensor_n):
            total = total + ref[c, t, low : low + 8, :]
        return jnp.sum(total, axis=0, keepdims=True)

    def multiply(c, owner, first):
        at = pl.multiple_of(owner * rows, 16)
        held = g[c, pl.ds(at, rows), :]

        def step(i, _):
            band = pl.ds(pl.multiple_of(i * band_rows, 16), band_rows)
            product = jnp.dot(
                w[band, pl.ds(pl.multiple_of(owner * rows, LANES), rows)],
                held,
                preferred_element_type=jnp.float32,
            )
            acc[c % 2, band, :] = product if first else acc[c % 2, band, :] + product
            return 0

        lax.fori_loop(0, rows // band_rows, step, 0)

    def both(c, j):
        @pl.when(me - j >= 0)
        def _():
            multiply(c, me - j, False)

        @pl.when(me + j < tensor_n)
        def _():
            multiply(c, me + j, False)

    def multiply_all(c):
        def step(i, _):
            band = pl.ds(pl.multiple_of(i * tile, 16), tile)
            acc[c % 2, band, :] = jnp.dot(
                w[band, :], g[c], preferred_element_type=jnp.float32
            )
            return 0

        lax.fori_loop(0, tiles, step, 0)

    def finish(c, hand):
        each(1, tensor_n, lambda d: square_copy(c, around(d), around(d), d).wait_recv())
        q = lax.rsqrt(over_tensor(sq, c, 0) / width + epsilon)

        def step(i, totals):
            at = pl.multiple_of(i * tile, 16)
            mixed = q * acc[c % 2, pl.ds(at, tile), :]
            v = x[c, pl.ds(at, tile), :].astype(jnp.float32)
            result = (v + mixed / (1.0 + jnp.exp(-mixed))).astype(jnp.bfloat16)
            o[c, pl.ds(at, tile), :] = result
            if hand:
                handoff(c, i).start()
            f = result.astype(jnp.float32)
            head = cols_ref[pl.ds(at, tile), 1:2]
            return totals[0] + folded(f * f), totals[1] + folded(f * head)

        zero = jnp.zeros((8, LANES), jnp.float32)
        squares, dots = lax.fori_loop(0, tiles, step, (zero, zero))
        parts[c, me, 0:8, :] = squares
        parts[c, me, 8:16, :] = dots
        store_out(c).start()
        if not hand:
            each(1, tensor_n, lambda d: part_copy(c, me, around(d), d).start())

    whole = rows % LANES != 0

    def begin(c):
        if not whole:
            multiply(c, me, True)

    def add(c, j):
        if not whole:
            both(c, j)

    def close(c, hand):
        if whole:
            multiply_all(c)
        finish(c, hand)

    turn = max(1, tensor_n - 2)

    def run(c, hand, meet, then=None):
        begin(c)

        def step(j, _):
            meet(j)
            if then:
                pl.when(j == turn)(then)
            add(c, j)
            return 0

        lax.fori_loop(1, tensor_n, step, 0)
        close(c, hand)

    assert chunks == 4
    last = chunks - 1

    @pl.when(sec == 0)
    def _():
        prepare(0, False)
        send(0)
        load_w.wait()

        def then0():
            prepare(2, False)
            send(2)
            prepare(1, False)
            start_squares(1)

        run(0, True, lambda j: arrived(0, j), then0)

        def meet1(j):
            pl.when(j == 1)(lambda: arrived(2, 1))
            crossed(1, j)

        run(1, True, meet1)

        def then2():
            prepare(3, False)
            send(3)

        run(2, True, lambda j: pl.when(j > 1)(lambda: arrived(2, j)), then2)
        run(3, True, lambda j: arrived(3, j))
        lend(last)
        for c in (0, 2, 3):
            wait_hops(hops(c))

    @pl.when(sec == 1)
    def _():
        load_tok(1, o).wait()
        lend(1)
        prepare(0, True)
        send(0)
        load_w.wait()
        for c in range(last - 1):

            def then(c=c + 1):
                prepare(c, True)
                send(c)

            run(c, False, lambda j: arrived(c, j), then)

        c = last - 1
        begin(c)

        def step(j, _):
            arrived(c, j)
            add(c, j)

            @pl.when(j == turn)
            def _():
                prepare(last, True)
                start_squares(last)
                begin(last)

            @pl.when(j > turn)
            def _():
                def catch_up(k, _):
                    crossed(last, k)
                    add(last, k)
                    return 0

                lax.fori_loop(1, turn + 1, catch_up, 0)

            return 0

        lax.fori_loop(1, tensor_n, step, 0)
        close(c, False)
        crossed(last, tensor_n - 1)
        add(last, tensor_n - 1)
        close(last, False)
        for c in (0, 1, 2):
            wait_hops(hops(c))

    @pl.when(sec == 1)
    def _():
        segment = lax.broadcasted_iota(jnp.int32, (SEGS, LANES), 0)
        for m in range(micros):
            losses = jnp.zeros((SEGS, LANES), jnp.float32)
            counts = jnp.zeros((SEGS, LANES), jnp.float32)
            for h in range(per_micro):
                c = m * per_micro + h
                each(
                    1,
                    tensor_n,
                    lambda d: part_copy(c, around(d), around(d), d).wait_recv(),
                )
                cut = slice(h * LANES, (h + 1) * LANES)
                inv_root = lax.rsqrt(over_tensor(parts, c, 0) / width + epsilon)
                scores = over_tensor(parts, c, 8) * inv_root
                weight = mask_ref[m : m + 1, cut].astype(jnp.float32)
                off = scores - (labels_ref[m : m + 1, cut].astype(jnp.float32) - 1.0)
                member = seg_ref[m : m + 1, cut] == segment
                losses += jnp.where(member, weight * off * off, 0.0)
                counts += jnp.where(member, weight, 0.0)
            lc[dp, m * SEGS : (m + 1) * SEGS, :] = losses
            lc[dp, (micros + m) * SEGS : (micros + m + 1) * SEGS, :] = counts
        each(1, group, lambda k: loss_copy(dp, k).start())
        each(1, dp_n, lambda k: loss_copy(lax.rem(dp + k, dp_n), k).wait_recv())

    @pl.when(sec == 0)
    def _():
        each(0, dp_n, lambda k: loss_copy(lax.rem(dp + k, dp_n), 1 + k).wait_recv())

    total = lc[0]
    for k in range(1, dp_n):
        total = total + lc[k]
    total = jnp.sum(total, axis=1, keepdims=True)
    half = micros * SEGS
    loss = total[:half] / jnp.maximum(total[half:], 1.0)
    lane = lax.broadcasted_iota(jnp.int32, (SEGS, LANES), 1)
    diagonal = lane == lax.broadcasted_iota(jnp.int32, (SEGS, LANES), 0)
    for m in range(micros):
        column = jnp.broadcast_to(loss[m * SEGS : (m + 1) * SEGS], (SEGS, LANES))
        row = jnp.sum(jnp.where(diagonal, column, 0.0), axis=0, keepdims=True)
        loss_ref[m : m + 1, :] = row[:, :SEGS]

    for c in range(chunks):
        each(1, tensor_n, lambda d: square_copy(c, me, around(d), d).wait_send())
        store_out(c).wait()
    wait_hops(lent)
    for h in range(PIECES):
        each(1, tensor_n, lambda d: cross(1, around(d), h).wait_send())
    gain_copy.wait_send()

    @pl.when(sec == 0)
    def _():
        for c in range(chunks):
            each(0, tiles, lambda i: handoff(c, i).wait_send())

    @pl.when(sec == 1)
    def _():
        for c in range(chunks):
            each(1, tensor_n, lambda d: part_copy(c, me, around(d), d).wait_send())
        each(1, group, lambda k: loss_copy(dp, k).wait_send())


def body(
    tensor_n,
    dp_n,
    tokens_in,
    section_proj,
    section_gain,
    final_gain,
    score_weight,
    labels,
    loss_mask,
    segment_ids,
):
    micros, rows, tokens = tokens_in.shape
    width = section_proj.shape[2]
    chunks = micros * (tokens // LANES)
    cols = jnp.stack(
        [
            section_gain[0].astype(jnp.float32),
            final_gain.astype(jnp.float32) * score_weight.astype(jnp.float32),
        ],
        axis=1,
    )
    dma = pltpu.SemaphoreType.DMA
    vmem = pl.BlockSpec(memory_space=pltpu.VMEM)
    hbm = pl.BlockSpec(memory_space=pl.ANY)
    out, loss = pl.pallas_call(
        functools.partial(kernel, tensor_n, dp_n, micros, width, rows),
        out_shape=(
            jax.ShapeDtypeStruct((micros, rows, tokens), jnp.bfloat16),
            jax.ShapeDtypeStruct((micros, SEGS), jnp.float32),
        ),
        in_specs=[hbm, hbm, vmem, vmem, vmem, vmem],
        out_specs=(hbm, vmem),
        scratch_shapes=[
            pltpu.VMEM((rows, width), jnp.bfloat16),
            pltpu.VMEM((chunks, rows, LANES), jnp.bfloat16),
            pltpu.VMEM((chunks, width, LANES), jnp.bfloat16),
            pltpu.VMEM((chunks, tensor_n, 8, LANES), jnp.float32),
            pltpu.VMEM((chunks, rows, LANES), jnp.bfloat16),
            pltpu.VMEM((2, rows, LANES), jnp.float32),
            pltpu.VMEM((rows, LANES), jnp.bfloat16),
            pltpu.VMEM((rows, LANES), jnp.bfloat16),
            pltpu.VMEM((width, LANES), jnp.bfloat16),
            pltpu.VMEM((chunks, tensor_n, 16, LANES), jnp.float32),
            pltpu.VMEM((dp_n, 2 * micros * SEGS, LANES), jnp.float32),
            dma,
            dma((chunks,)),
            dma((chunks,)),
            dma((chunks, tensor_n + 1, PIECES)),
            dma((chunks, tensor_n, PIECES)),
            dma((chunks, tensor_n)),
            dma((chunks, tensor_n)),
            dma((chunks, rows // row_tile(rows))),
            dma((chunks, rows // row_tile(rows))),
            dma((chunks, tensor_n)),
            dma((chunks, tensor_n)),
            dma((2 * dp_n,)),
            dma((dp_n,)),
            dma((tensor_n + 1, PIECES)),
            dma((tensor_n, PIECES)),
            dma((tensor_n, PIECES)),
            dma,
            dma,
        ],
        compiler_params=pltpu.CompilerParams(
            collective_id=0, has_side_effects=True, vmem_limit_bytes=56 * 2**20
        ),
        cost_estimate=pl.CostEstimate(
            flops=2 * rows * width * micros * tokens,
            bytes_accessed=2 * rows * width,
            transcendentals=0,
        ),
        name="relay",
    )(tokens_in, section_proj[0], cols, labels, loss_mask, segment_ids)
    return out[None], loss


def solution(mesh):
    in_specs = (
        P(None, "tensor", "dp"),
        P("section", "tensor", None),
        P("section", "tensor"),
        P("tensor"),
        P("tensor"),
        P(None, "dp"),
        P(None, "dp"),
        P(None, "dp"),
    )
    out_specs = (P("section", None, "tensor", "dp"), P())
    return jax.shard_map(
        functools.partial(body, mesh.shape["tensor"], mesh.shape["dp"]),
        mesh=mesh,
        in_specs=in_specs,
        out_specs=out_specs,
        check_vma=False,
    )
```
